256 devices in a mesh: ccd: 64 (over z, x, core), tile: 4 (over y).
Axes of the slice: x: 4, y: 4, z: 8, core: 2. Of those that a mesh axis runs over, the one named last changes fastest.
Arguments:
- visit_image: bfloat16 [32768, 1024], P(('ccd', 'tile')), may hold values from -6 to 6
- mask_bits: int32 [32768, 1024], P(('ccd', 'tile')), may hold values from 0 to 15
- visit_weight: float32 [64], P('ccd'), may hold values from 1 to 4
- basis_cols: bfloat16 [31, 21], replicated, may hold values from -1.25 to 1.25
- basis_rows: bfloat16 [31, 21], replicated, may hold values from -1.25 to 1.25
- kernel_coef: float32 [64, 31, 6], P('ccd'), may hold values from -1 to 1
- row_warp: bfloat16 [32768, 512], P(('ccd', 'tile')), may hold values from -1 to 1, as said below
- col_warp: bfloat16 [64, 1024, 1024], P('ccd'), may hold values from -1 to 1, as said below
- dest_owner: int32 [16384, 1], P(('ccd', 'tile')), may hold values from 0 to 63; in each aligned block of 64 rows (0 to 63, 64 to 127, ...) at most 2 rows name the same one
- dest_block: int32 [16384], P(('ccd', 'tile')), may hold values from 0 to 63
- new_science: float32 [32768, 1024], P(('ccd', 'tile')), may hold values from -6 to 6
- tmpl_owner: int32 [16384, 1], P(('ccd', 'tile')), may hold values from 0 to 63; in each aligned block of 64 rows (0 to 63, 64 to 127, ...) at most 2 rows name the same one
- tmpl_block: int32 [16384], P(('ccd', 'tile')), may hold values from 0 to 63
Outputs:
- coadd: float32 [32768, 1024], P(('ccd', 'tile'))
- difference: float32 [32768, 1024], P(('ccd', 'tile'))
The draws below stay inside these ranges and needn't reach their ends.
Inputs may be any that keep to these rules, and one draw needn't show every extreme that they name: `dest_owner`: within the 64 rows of one device no patch is named more than 2 times, a bound that some block reaches. `tmpl_owner`: within the 64 rows of one device no patch is named more than 2 times, a bound that some block reaches. `row_warp`: Lanczos-3 interpolation weights for a dither of 0 or plus or minus 512 / 2 rows plus a shift within 8 pixels, and a scale change within 3 / 512; rows that fall off the cutout are zero. `col_warp`: Lanczos-3 interpolation weights for a shift within 8 pixels and a scale change within 3 / 1024; every nonzero lies within 14 of the diagonal.
All inputs are finite; a program needn't handle non-finite values.
Results may differ from the reference program's by a relative error of at most 0.015.
Values may be sent and summed in bfloat16 or wider, within the bound.
No kernel may reach another device: no remote copies, remote signals or barrier semaphores. Data moves between devices by JAX's collectives and lax.ppermute only.
A program may use at most 192 MiB of HBM per device.

```python
import math
import jax
import jax.numpy as jnp
import numpy as np
from jax import lax

W = 1024
ROWS_DEV = 128
NB = 31
KT = 21
NPOLY = 6
BLOCK_ROWS = 16
BLOCK_COLUMNS = 128
CH = 512
ROWS = 32768
NBLK = 64
CAP = 2
ALLBLK = 16384
N_CCD = 64
N_TILE = 4


def lanczos_weight(offset):
    inside = jnp.abs(offset) < 3.0
    return jnp.where(inside, jnp.sinc(offset) * jnp.sinc(offset / 3.0), 0.0)


def draw_row_warp(key, part):
    key_shift, key_scale, key_dither = jax.random.split(jax.random.fold_in(key, 11), 3)
    shift = jax.random.uniform(key_shift, (N_CCD, 1, 1), jnp.float32, -8.0, 8.0)
    dither = jax.random.randint(key_dither, (N_CCD,), -1, 2)
    dither = jnp.where(jnp.arange(N_CCD) == 0, 1, dither).astype(jnp.float32)
    shift = shift + (dither * (CH // 2)).reshape(N_CCD, 1, 1)
    scale = jax.random.uniform(key_scale, (N_CCD, 1, 1), jnp.float32, -3.0 / CH, 3.0 / CH)
    outs = jnp.arange(CH, dtype=jnp.float32)[None, :, None]
    ins = jnp.arange(CH, dtype=jnp.float32)[None, None, :]
    mats = lanczos_weight(ins - (outs * (1.0 + scale) + shift))
    return mats.reshape(N_CCD * CH, CH).astype(jnp.bfloat16)


def draw_col_warp(key, part):
    key_shift, key_scale = jax.random.split(jax.random.fold_in(key, 23))
    shift = jax.random.uniform(key_shift, (N_CCD, 1, 1), jnp.float32, -8.0, 8.0)
    scale = jax.random.uniform(key_scale, (N_CCD, 1, 1), jnp.float32, -3.0 / W, 3.0 / W)
    ins = jnp.arange(W, dtype=jnp.float32)[None, :, None]
    outs = jnp.arange(W, dtype=jnp.float32)[None, None, :]
    mats = lanczos_weight(ins - (outs * (1.0 + scale) + shift))
    return mats.astype(jnp.bfloat16)


def touch_ends(drawn, own_key, least, high):
    index_at = [jax.random.randint(jax.random.fold_in(own_key, axis), (), 0, length) for axis, length in enumerate(drawn.shape)]
    main_axis = drawn.shape.index(max(drawn.shape))
    beside = index_at[:main_axis] + [(index_at[main_axis] + 1) % drawn.shape[main_axis]] + index_at[main_axis + 1:]
    return drawn.at[tuple(index_at)].set(least).at[tuple(beside)].set(high)


def levels(own_key, dims, pieces, smallest, largest):
    def one(dim, shards_of):
        heights = jax.random.uniform(jax.random.fold_in(jax.random.fold_in(own_key, 6), dim), (shards_of,), jnp.float32, smallest / len(pieces), largest / len(pieces))
        return jnp.repeat(jnp.exp(heights), dims[dim] // shards_of).reshape((-1,) + (1,) * (len(dims) - dim - 1))

    gain = one(*pieces[0])
    for cut in pieces[1:]:
        gain = gain * one(*cut)
    return gain


def deal_out(key, own, number, rows, amount, top, bound, slope):
    order = jax.random.permutation(key, amount)
    crowded, usual = shares(amount, rows * top, bound, slope, True), shares(amount, rows * top, bound, slope, False)
    places = jnp.arange(amount)

    def named(lengths, turn):
        used = int((lengths > 0).sum())
        fixed = max(1, used // 4)
        moved = fixed + (places - fixed + turn * (used - fixed)) % max(1, amount - fixed)
        return jnp.zeros((amount,), jnp.int32).at[order[jnp.where(places < fixed, places, moved)]].set(jnp.asarray(lengths, jnp.int32))

    lengths = jnp.where(number % 4 == 0, named(crowded, number // 4), named(usual, number - number // 4 - 1))
    mixed = jax.random.permutation(jax.random.fold_in(own, 3), amount)
    source_of, receiver = mixed[0:amount // 2 * 2:2], mixed[1:amount // 2 * 2:2]
    margin = jnp.minimum(lengths[source_of] - 1, bound - lengths[receiver]) // 2
    margin = jnp.where((source_of == order[0]) | (receiver == order[0]) | (lengths[receiver] == 0), 0, jnp.maximum(margin, 0))
    moved = jax.random.randint(jax.random.fold_in(own, 4), (amount // 2,), 0, 1 << 20) % (margin + 1)
    lengths = lengths.at[source_of].add(-moved).at[receiver].add(moved)
    members = jnp.searchsorted(jnp.cumsum(lengths), jnp.arange(rows * top), side="right").astype(jnp.int32)
    grid = members.reshape(top, rows).T
    grid = grid[jax.random.permutation(jax.random.fold_in(own, 1), rows)]
    turn = jax.random.randint(jax.random.fold_in(own, 2), (rows, 1), 0, top)
    return jnp.take_along_axis(grid, (jnp.arange(top)[None, :] + turn) % top, axis=1)


def shares(amount, total, limit, slope, full):
    portions = [(1 << 20) // math.isqrt(rank ** slope) + 1 for rank in range(1, amount + 1)]
    largest = limit if full else min(limit, max(-(-total // amount), total * portions[0] // sum(portions)))
    least = 1 if total - largest >= amount - 1 else 0
    given, spare = [largest] + [least] * (amount - 1), total - largest - least * (amount - 1)
    while spare > 0:
        free = [i for i in range(1, amount) if given[i] < largest] or [i for i in range(1, amount) if given[i] < limit]
        whole, left = sum([portions[i] for i in free]), spare
        for i in free:
            more = min(limit - given[i], max(1, left * portions[i] // whole), spare)
            given[i] = given[i] + more
            spare = spare - more
    return np.array(given)


def centred(rng, extent, scale, reach, pieces=(), held_as=jnp.bfloat16):
    array = jax.random.normal(rng, extent, jnp.float32) * scale
    if len(pieces) > 0:
        array = levels(rng, extent, pieces, -0.22, 0.18) * array
    return jnp.clip(array, min=-reach, max=reach).astype(held_as)


def setup_inputs(seed: int = 0) -> dict:
    seeds = jax.random.split(jax.random.key(seed), 14)
    visit_image = centred(seeds[0], (ROWS, W), 1.0, 6.0, ((0, 256),))
    mask_bits = touch_ends(jax.random.randint(seeds[1], (ROWS, W), 0, 16), jax.random.fold_in(seeds[1], 1), 0, 15).astype(jnp.int32)
    visit_weight = jnp.clip(jnp.exp(math.log(4.0) - 1.3862944 * jax.random.uniform(seeds[2], (N_CCD,), jnp.float32) ** levels(seeds[2], (N_CCD,), ((0, 64),), -0.2, 0.2)), 1.0, 4.0)
    basis_cols = centred(seeds[3], (NB, KT), KT ** -0.5, 1.25)
    basis_rows = centred(seeds[4], (NB, KT), KT ** -0.5, 1.25)
    kernel_coef = centred(seeds[5], (N_CCD, NB, NPOLY), NB ** -0.5, 1.0, ((0, 64),), jnp.float32)
    row_warp = draw_row_warp(jax.random.fold_in(seeds[13], 71), 0)
    col_warp = draw_col_warp(jax.random.fold_in(seeds[13], 71), 0)
    dest_owner_keys = jax.random.split(jax.random.fold_in(seeds[8], 1), ALLBLK // NBLK)
    dest_owner_turns = jax.random.permutation(jax.random.fold_in(seeds[8], 3), ALLBLK // NBLK)
    dest_owner = jax.vmap(lambda own, number: deal_out(jax.random.fold_in(seeds[8], 2), own, number, NBLK, N_CCD, 1, CAP, 2))(dest_owner_keys, dest_owner_turns).reshape((ALLBLK, 1))
    dest_block = touch_ends(jax.random.randint(seeds[9], (ALLBLK,), 0, NBLK), jax.random.fold_in(seeds[9], 1), 0, NBLK - 1).astype(jnp.int32)
    new_science = centred(seeds[10], (ROWS, W), 1.0, 6.0, ((0, 256),), jnp.float32)
    tmpl_owner_keys = jax.random.split(jax.random.fold_in(seeds[11], 1), ALLBLK // NBLK)
    tmpl_owner_turns = jax.random.permutation(jax.random.fold_in(seeds[11], 3), ALLBLK // NBLK)
    tmpl_owner = jax.vmap(lambda own, number: deal_out(jax.random.fold_in(seeds[11], 2), own, number, NBLK, N_CCD, 1, CAP, 2))(tmpl_owner_keys, tmpl_owner_turns).reshape((ALLBLK, 1))
    tmpl_block = touch_ends(jax.random.randint(seeds[12], (ALLBLK,), 0, NBLK), jax.random.fold_in(seeds[12], 1), 0, NBLK - 1).astype(jnp.int32)
    return dict(visit_image=visit_image, mask_bits=mask_bits, visit_weight=visit_weight, basis_cols=basis_cols, basis_rows=basis_rows, kernel_coef=kernel_coef, row_warp=row_warp, col_warp=col_warp, dest_owner=dest_owner, dest_block=dest_block, new_science=new_science, tmpl_owner=tmpl_owner, tmpl_block=tmpl_block)


FLOOR = 1.0


def poly_planes(nrows, width):
    ys = (2.0 * jnp.arange(nrows, dtype=jnp.float32) + 1.0) / nrows - 1.0
    xs = (2.0 * jnp.arange(width, dtype=jnp.float32) + 1.0) / width - 1.0
    yy = ys[:, None] + jnp.zeros((1, width), jnp.float32)
    xx = xs[None, :] + jnp.zeros((nrows, 1), jnp.float32)
    return jnp.stack([jnp.ones_like(yy), yy, xx, yy * yy, yy * xx, xx * xx])


def convolve_ccd(image, coef, basis_cols, basis_rows):
    half = (KT - 1) // 2
    ext = jnp.pad(image.astype(jnp.float32), ((half, half), (0, 0)))
    colsf = basis_cols.astype(jnp.float32)
    rowsf = basis_rows.astype(jnp.float32)
    vert = jnp.zeros((NB, CH, W), jnp.float32)
    for j in range(KT):
        vert = vert + colsf[:, j, None, None] * ext[None, j:j + CH, :]
    vert = lax.optimization_barrier(vert.astype(jnp.bfloat16)).astype(jnp.float32)
    padded = jnp.pad(vert, ((0, 0), (0, 0), (half, half)))
    horiz = jnp.zeros((NB, CH, W), jnp.float32)
    for i in range(KT):
        horiz = horiz + rowsf[:, i, None, None] * padded[:, :, i:i + W]
    mixed = jnp.einsum("bp,brx->prx", coef, horiz, precision=lax.Precision.HIGHEST)
    return jnp.sum(mixed * poly_planes(CH, W), axis=0)


def reference(visit_image, mask_bits, visit_weight, basis_cols, basis_rows, kernel_coef, row_warp, col_warp, dest_owner, dest_block, new_science, tmpl_owner, tmpl_block):
    images = visit_image.reshape(N_CCD, CH, W)
    masks = mask_bits.reshape(N_CCD, CH, W)
    rowmats = row_warp.reshape(N_CCD, CH, CH)

    def per_ccd(items):
        image, mask, weight, coef, rowmat, colmat = items
        conv = convolve_ccd(image, coef, basis_cols, basis_rows)
        bad = jnp.bitwise_and(mask, 3) == 3
        wplane = jnp.where(bad, jnp.zeros_like(conv), weight + jnp.zeros_like(conv)).astype(jnp.bfloat16)
        flux = (wplane.astype(jnp.float32) * conv).astype(jnp.bfloat16)
        planes = jnp.stack([flux, wplane]).astype(jnp.float32)
        rowed = jnp.einsum("rs,psx->prx", rowmat.astype(jnp.float32), planes, precision=lax.Precision.HIGHEST)
        rowed = lax.optimization_barrier(rowed.astype(jnp.bfloat16)).astype(jnp.float32)
        return jnp.einsum("prx,xy->pry", rowed, colmat.astype(jnp.float32), precision=lax.Precision.HIGHEST)

    warped = lax.map(per_ccd, (images, masks, visit_weight, kernel_coef, rowmats, col_warp))
    blocks = warped.reshape(N_CCD, 2, N_TILE, ROWS_DEV // BLOCK_ROWS, BLOCK_ROWS, W // BLOCK_COLUMNS, BLOCK_COLUMNS)
    blocks = blocks.transpose(0, 2, 3, 5, 1, 4, 6).reshape(N_CCD, N_TILE, NBLK, 2, BLOCK_ROWS, BLOCK_COLUMNS)
    owners = dest_owner.reshape(N_CCD, N_TILE, NBLK).astype(jnp.int32)
    targets = dest_block.reshape(N_CCD, N_TILE, NBLK).astype(jnp.int32)
    tiles = (jnp.zeros((N_CCD, N_TILE, NBLK), jnp.int32) + jnp.arange(N_TILE, dtype=jnp.int32)[None, :, None])
    acc = jnp.zeros((N_CCD, N_TILE, NBLK, 2, BLOCK_ROWS, BLOCK_COLUMNS), jnp.float32).at[owners, tiles, targets].add(blocks)
    coadd_blocks = acc[:, :, :, 0] / jnp.maximum(acc[:, :, :, 1], FLOOR)
    coadd = coadd_blocks.reshape(N_CCD, N_TILE, ROWS_DEV // BLOCK_ROWS, W // BLOCK_COLUMNS, BLOCK_ROWS, BLOCK_COLUMNS).transpose(0, 1, 2, 4, 3, 5).reshape(ROWS, W)
    towners = tmpl_owner.reshape(N_CCD, N_TILE, NBLK).astype(jnp.int32)
    tblocks = tmpl_block.reshape(N_CCD, N_TILE, NBLK).astype(jnp.int32)
    template = coadd_blocks[towners, tiles, tblocks]
    template = template.reshape(N_CCD, N_TILE, ROWS_DEV // BLOCK_ROWS, W // BLOCK_COLUMNS, BLOCK_ROWS, BLOCK_COLUMNS).transpose(0, 1, 2, 4, 3, 5).reshape(ROWS, W)
    return coadd, new_science - template
```

```python
import functools

import jax
import jax.numpy as jnp
from jax import lax
from jax.experimental import pallas as pl
from jax.experimental.pallas import tpu as pltpu
from jax.sharding import PartitionSpec as P

BLOCK_ROWS = 16
BLOCK_COLUMNS = 128
FLOOR = 1.0

ROWS = 128
WIDTH = 1024
CUTOUT = 512
NTILE = 4
NB = 31
TAPS = 21
HALF = 10
EDGE = 16
BAND = 64
WINDOW = 96
DEPTH = 2048
USED = TAPS * WINDOW
NBLK = 64
SLOTS = 128

VMEM = pl.BlockSpec(memory_space=pltpu.VMEM)
SMEM = pl.BlockSpec(memory_space=pltpu.SMEM)


def call(body, out_shape, in_specs, out_specs, scratch, name, flops, nbytes):
    return pl.pallas_call(
        body,
        out_shape=out_shape,
        in_specs=in_specs,
        out_specs=out_specs,
        scratch_shapes=scratch,
        name=name,
        compiler_params=pltpu.CompilerParams(vmem_limit_bytes=40 * 1024 * 1024),
        cost_estimate=pl.CostEstimate(flops=flops, bytes_accessed=nbytes, transcendentals=0),
    )


def index_kernel(dest_owner, dest_block, tmpl_owner, tmpl_block, dest_slot, tmpl_slot, table, count):
    def clear(i, _):
        count[i] = 0
        count[64 + i] = 0
        table[4 * i] = NBLK
        table[4 * i + 1] = NBLK
        table[4 * i + 2] = 0
        table[4 * i + 3] = 0
        return 0

    lax.fori_loop(0, 64, clear, 0, unroll=8)

    def place(k, _):
        owner = dest_owner[k]
        rank = count[owner]
        count[owner] = rank + 1
        dest_slot[k] = 2 * owner + rank
        table[4 * owner + rank] = dest_block[k]
        asked = tmpl_owner[k]
        rank = count[64 + asked]
        count[64 + asked] = rank + 1
        tmpl_slot[k] = 2 * asked + rank
        table[4 * asked + 2 + rank] = tmpl_block[k]
        return 0

    lax.fori_loop(0, 64, place, 0, unroll=8)


def table_kernel(tile, coef, cols, rows_t, table):
    taps = []
    for p in range(6):
        taps.append(
            jnp.dot(
                rows_t[...],
                coef[:, p : p + 1] * cols[...],
                preferred_element_type=jnp.float32,
                precision=lax.Precision.HIGHEST,
            )
        )
    lane = lax.broadcasted_iota(jnp.int32, (BAND, 128), 1)
    row = lax.broadcasted_iota(jnp.int32, (BAND, 128), 0)
    for band in range(2):
        first = tile[0] * ROWS + band * BAND
        yn = (2.0 * (first + row).astype(jnp.float32) + 1.0) / CUTOUT - 1.0
        yy = yn * yn

        def turned(i):
            v = [jnp.broadcast_to(taps[p][i : i + 1, :], (BAND, 128)) for p in range(6)]
            mixed = (v[0] + yn * v[1] + yy * v[3], v[2] + yn * v[4], v[5])
            return [
                pltpu.roll(m, (i * WINDOW) % 128, 1, stride=1, stride_axis=0) for m in mixed
            ]

        held = {}
        for column in range(DEPTH // 128):
            left = (128 * column) // WINDOW
            bound = (left + 1) * WINDOW - 128 * column
            for i in (left, left + 1):
                if i < TAPS and i not in held:
                    held[i] = turned(i)
            for q in range(3):
                other = held[left + 1][q] if left + 1 < TAPS else jnp.zeros((BAND, 128), jnp.float32)
                table[band, q * BAND : (q + 1) * BAND, column * 128 : (column + 1) * 128] = jnp.where(
                    lane < bound, held[left][q], other
                ).astype(jnp.bfloat16)
            held = {i: held[i] for i in held if i > left}


def conv_kernel(visit_weight, top, image, bottom, table, mask, planes, edges, stack):
    for group in range(10):
        if group == 0:
            strip = top[...]
        elif group == 9:
            strip = bottom[...]
        else:
            strip = image[(group - 1) * 16 : group * 16, :]
        strip = jnp.concatenate(
            [strip.astype(jnp.float32), jnp.zeros((16, 128), jnp.float32)], axis=1
        )
        for i in range(TAPS):
            moved = strip if i == HALF else pltpu.roll(strip, (HALF - i) % (WIDTH + 128), 1)
            moved = moved[:, :WIDTH].astype(jnp.bfloat16)
            if group < 6:
                at = i * WINDOW + group * 16
                stack[0, at : at + 16, :] = moved
            if group >= 4:
                at = i * WINDOW + group * 16 - BAND
                stack[1, at : at + 16, :] = moved
    stack[:, USED:, :] = jnp.zeros((2, DEPTH - USED, WIDTH), jnp.bfloat16)
    scale = visit_weight[0].astype(jnp.bfloat16).astype(jnp.float32)
    for band in range(2):
        rows = slice(band * BAND, (band + 1) * BAND)
        for n in range(4):
            columns = slice(n * 256, (n + 1) * 256)
            parts = jnp.dot(
                table[band], stack[band, :, columns], preferred_element_type=jnp.float32
            )
            x = lax.broadcasted_iota(jnp.int32, (BAND, 256), 1) + n * 256
            xn = (2.0 * x.astype(jnp.float32) + 1.0) / WIDTH - 1.0
            conv = parts[:BAND] + xn * (parts[BAND : 2 * BAND] + xn * parts[2 * BAND :])
            bad = jnp.bitwise_and(mask[rows, columns], 3) == 3
            weight = jnp.where(bad, 0.0, scale)
            planes[0, rows, columns] = (weight * conv).astype(jnp.bfloat16)
            planes[1, rows, columns] = weight.astype(jnp.bfloat16)
    edges[:, :EDGE, :] = planes[:, :EDGE, :]
    edges[:, EDGE:, :] = planes[:, ROWS - EDGE :, :]


def warp_kernel(
    tile, dest_slot, planes, far, after, before, row_warp, col_warp, outgoing, cutout, rowed
):
    t = tile[0]
    for block, edges in ((lax.rem(t + 1, NTILE), after), (lax.rem(t + 3, NTILE), before)):
        start = pl.multiple_of(block * ROWS, ROWS)
        cutout[:, pl.ds(start + EDGE, ROWS - 2 * EDGE), :] = jnp.zeros(
            (2, ROWS - 2 * EDGE, WIDTH), jnp.bfloat16
        )
        cutout[:, pl.ds(start, EDGE), :] = edges[:, :EDGE, :]
        cutout[:, pl.ds(start + ROWS - EDGE, EDGE), :] = edges[:, EDGE:, :]
    cutout[:, pl.ds(pl.multiple_of(t * ROWS, ROWS), ROWS), :] = planes[...]
    cutout[:, pl.ds(pl.multiple_of(lax.rem(t + 2, NTILE) * ROWS, ROWS), ROWS), :] = far[...]
    for plane in range(2):
        rowed[plane * ROWS : (plane + 1) * ROWS, :] = jnp.dot(
            row_warp[...], cutout[plane], preferred_element_type=jnp.float32
        ).astype(jnp.bfloat16)
    for n in range(4):
        low, high = max(0, 256 * n - 128), min(WIDTH, 256 * n + 384)
        warped = jnp.dot(
            rowed[:, low:high],
            col_warp[low:high, 256 * n : 256 * n + 256],
            preferred_element_type=jnp.float32,
        ).astype(jnp.bfloat16)
        for down in range(8):
            for c in range(2):
                slot = dest_slot[down * 8 + 2 * n + c]
                rows = slice(down * 16, down * 16 + 16)
                columns = slice(c * 128, c * 128 + 128)
                outgoing[slot, :16, :] = warped[:ROWS][rows, columns]
                outgoing[slot, 16:, :] = warped[ROWS:][rows, columns]


def patch_kernel(table, arriving, coadd, reply, sums, served):
    sums[...] = jnp.zeros_like(sums)

    def add(patch, _):
        for rank in range(2):
            at = table[4 * patch + rank]
            sums[at] = sums[at] + arriving[2 * patch + rank].astype(jnp.float32)
        return 0

    lax.fori_loop(0, 64, add, 0, unroll=4)
    for block in range(NBLK):
        down, c = block // 8, block % 8
        value = sums[block, :16, :] / jnp.maximum(sums[block, 16:, :], FLOOR)
        coadd[down * 16 : down * 16 + 16, c * 128 : c * 128 + 128] = value
        served[block] = value.astype(jnp.bfloat16)

    def serve(patch, _):
        for rank in range(2):
            reply[2 * patch + rank] = served[table[4 * patch + 2 + rank]]
        return 0

    lax.fori_loop(0, 64, serve, 0, unroll=4)


def difference_kernel(tmpl_slot, returned, new_science, difference):
    for block in range(NBLK):
        down, c = block // 8, block % 8
        at = (slice(down * 16, down * 16 + 16), slice(c * 128, c * 128 + 128))
        difference[at] = new_science[at] - returned[tmpl_slot[block]].astype(jnp.float32)


def per_device(
    visit_image,
    mask_bits,
    visit_weight,
    basis_cols,
    basis_rows,
    kernel_coef,
    row_warp,
    col_warp,
    dest_owner,
    dest_block,
    new_science,
    tmpl_owner,
    tmpl_block,
):
    f32, bf16, i32 = jnp.float32, jnp.bfloat16, jnp.int32
    struct = jax.ShapeDtypeStruct
    tile = lax.axis_index("tile").astype(i32).reshape(1)
    up = [(i, (i + 1) % NTILE) for i in range(NTILE)]
    down = [(i, (i + 3) % NTILE) for i in range(NTILE)]
    across = [(i, (i + 2) % NTILE) for i in range(NTILE)]

    top = lax.ppermute(visit_image[ROWS - EDGE :], "tile", up[:-1])
    bottom = lax.ppermute(visit_image[:EDGE], "tile", down[1:])

    dest_slot, tmpl_slot, table = call(
        index_kernel,
        (struct((64,), i32), struct((64,), i32), struct((256,), i32)),
        [SMEM] * 4,
        (SMEM,) * 3,
        [pltpu.SMEM((128,), i32)],
        "slots",
        1000,
        4096,
    )(dest_owner[:, 0], dest_block, tmpl_owner[:, 0], tmpl_block)
    received = lax.all_to_all(
        table.reshape(64, 4), "ccd", split_axis=0, concat_axis=0, tiled=True
    ).reshape(256)

    cols = jnp.pad(basis_cols.astype(f32), ((0, 1), (6, 128 - 6 - TAPS)))
    rows_t = jnp.pad(basis_rows.astype(f32).T, ((0, 3), (0, 1)))
    coef = jnp.pad(kernel_coef[0], ((0, 1), (0, 0)))
    taps = call(
        table_kernel,
        struct((2, 3 * BAND, DEPTH), bf16),
        [SMEM, VMEM, VMEM, VMEM],
        VMEM,
        [],
        "taps",
        10_000_000,
        2_000_000,
    )(tile, coef, cols, rows_t)
    planes, edges = call(
        conv_kernel,
        (struct((2, ROWS, WIDTH), bf16), struct((2, 2 * EDGE, WIDTH), bf16)),
        [SMEM] + [VMEM] * 5,
        (VMEM, VMEM),
        [pltpu.VMEM((2, DEPTH, WIDTH), bf16)],
        "matching",
        2 * 2 * 192 * DEPTH * WIDTH,
        3_000_000,
    )(visit_weight, top, visit_image, bottom, taps, mask_bits)
    far = lax.ppermute(planes, "tile", across)
    after = lax.ppermute(edges, "tile", down)
    before = lax.ppermute(edges, "tile", up)
    outgoing = call(
        warp_kernel,
        struct((SLOTS, 32, 128), bf16),
        [SMEM, SMEM] + [VMEM] * 6,
        VMEM,
        [pltpu.VMEM((2, CUTOUT, WIDTH), bf16), pltpu.VMEM((2 * ROWS, WIDTH), bf16)],
        "warp",
        2 * 256 * WIDTH * WIDTH,
        5_000_000,
    )(tile, dest_slot, planes, far, after, before, row_warp, col_warp[0])
    arriving = lax.all_to_all(outgoing, "ccd", split_axis=0, concat_axis=0, tiled=True)
    coadd, reply = call(
        patch_kernel,
        (struct((ROWS, WIDTH), f32), struct((SLOTS, 16, 128), bf16)),
        [SMEM, VMEM],
        (VMEM, VMEM),
        [pltpu.VMEM((NBLK + 8, 32, 128), f32), pltpu.VMEM((NBLK, 16, 128), bf16)],
        "patch",
        1_000_000,
        2_000_000,
    )(received, arriving)
    returned = lax.all_to_all(reply, "ccd", split_axis=0, concat_axis=0, tiled=True)
    difference = call(
        difference_kernel,
        struct((ROWS, WIDTH), f32),
        [SMEM, VMEM, VMEM],
        VMEM,
        [],
        "difference",
        1_000_000,
        2_000_000,
    )(tmpl_slot, returned, new_science)
    return coadd, difference


def solution(mesh):
    both = P(("ccd", "tile"), None)
    return jax.shard_map(
        per_device,
        mesh=mesh,
        in_specs=(
            both,
            both,
            P("ccd"),
            P(),
            P(),
            P("ccd", None, None),
            both,
            P("ccd", None, None),
            both,
            P(("ccd", "tile")),
            both,
            both,
            P(("ccd", "tile")),
        ),
        out_specs=(both, both),
        check_vma=False,
    )
```

```python
import functools

import jax
import jax.numpy as jnp
from jax import lax
from jax.experimental import pallas as pl
from jax.experimental.pallas import tpu as pltpu
from jax.sharding import PartitionSpec as P

BLOCK_ROWS = 16
BLOCK_COLUMNS = 128
FLOOR = 1.0

ROWS = 128
WIDTH = 1024
CUTOUT = 512
NTILE = 4
NB = 31
TAPS = 21
HALF = 10
EDGE = 16
BAND = 64
WINDOW = 96
DEPTH = 2048
USED = TAPS * WINDOW
NBLK = 64
SLOTS = 128
NOTE = 8
MESSAGE = 64 + NOTE

VMEM = pl.BlockSpec(memory_space=pltpu.VMEM)
HBM = pl.BlockSpec(memory_space=pltpu.HBM)
SMEM = pl.BlockSpec(memory_space=pltpu.SMEM)


def in_hbm(array):
    return pltpu.with_memory_space_constraint(array, pltpu.HBM)


def call(body, out_shape, in_specs, out_specs, scratch, name, flops, nbytes):
    return pl.pallas_call(
        body,
        out_shape=out_shape,
        in_specs=in_specs,
        out_specs=out_specs,
        scratch_shapes=scratch,
        name=name,
        compiler_params=pltpu.CompilerParams(vmem_limit_bytes=40 * 1024 * 1024),
        cost_estimate=pl.CostEstimate(flops=flops, bytes_accessed=nbytes, transcendentals=0),
    )


def index_kernel(
    home,
    dest_owner,
    dest_block,
    tmpl_owner,
    tmpl_block,
    dest_slot,
    tmpl_slot,
    notes,
    count,
    table,
):
    def clear(i, _):
        count[i] = 0
        count[64 + i] = 0
        table[4 * i] = NBLK
        table[4 * i + 1] = NBLK
        table[4 * i + 2] = 0
        table[4 * i + 3] = 0
        return 0

    lax.fori_loop(0, 64, clear, 0, unroll=8)

    def place(k, _):
        owner = dest_owner[k]
        rank = count[owner]
        count[owner] = rank + 1
        dest_slot[k] = 2 * owner + rank
        table[4 * owner + rank] = dest_block[k]
        asked = tmpl_owner[k]
        rank = count[64 + asked]
        count[64 + asked] = rank + 1
        tmpl_slot[k] = 2 * asked + rank
        table[4 * asked + 2 + rank] = tmpl_block[k]
        return 0

    lax.fori_loop(0, 64, place, 0, unroll=8)

    row = lax.broadcasted_iota(jnp.int32, (NOTE, 128), 0)
    lane = lax.broadcasted_iota(jnp.int32, (NOTE, 128), 1) - 2 * home[0]
    for patch in range(64):
        note = jnp.zeros((NOTE, 128), jnp.int32)
        for kind in range(2):
            for rank in range(2):
                here = (row == kind) & (lane == rank)
                note = jnp.where(here, table[4 * patch + 2 * kind + rank], note)
        notes[patch] = note.astype(jnp.float32).astype(jnp.bfloat16)


def table_kernel(tile, coef, cols_t, rows_t, table, wide):
    wide[...] = jnp.zeros_like(wide)
    wide[6 : 6 + TAPS, :] = cols_t[...].astype(jnp.float32)
    taps = []
    for p in range(6):
        taps.append(
            lax.dot_general(
                rows_t[...].astype(jnp.float32) * coef[p],
                wide[...],
                (((1,), (1,)), ((), ())),
                preferred_element_type=jnp.float32,
                precision=lax.Precision.HIGHEST,
            )
        )
    lane = lax.broadcasted_iota(jnp.int32, (BAND, 128), 1)
    row = lax.broadcasted_iota(jnp.int32, (BAND, 128), 0)
    for band in range(2):
        first = tile[0] * ROWS + band * BAND
        yn = (2.0 * (first + row).astype(jnp.float32) + 1.0) / CUTOUT - 1.0
        yy = yn * yn

        def turned(i):
            v = [jnp.broadcast_to(taps[p][i : i + 1, :], (BAND, 128)) for p in range(6)]
            mixed = (v[0] + yn * v[1] + yy * v[3], v[2] + yn * v[4], v[5])
            return [
                pltpu.roll(m, (i * WINDOW) % 128, 1, stride=1, stride_axis=0) for m in mixed
            ]

        held = {}
        for column in range(DEPTH // 128):
            left = (128 * column) // WINDOW
            bound = (left + 1) * WINDOW - 128 * column
            for i in (left, left + 1):
                if i < TAPS and i not in held:
                    held[i] = turned(i)
            for q in range(3):
                other = held[left + 1][q] if left + 1 < TAPS else jnp.zeros((BAND, 128), jnp.float32)
                table[band, q * BAND : (q + 1) * BAND, column * 128 : (column + 1) * 128] = jnp.where(
                    lane < bound, held[left][q], other
                ).astype(jnp.bfloat16)
            held = {i: held[i] for i in held if i > left}


def good_weight(mask, scale):
    return jnp.where(jnp.bitwise_and(mask, 3) == 3, 0.0, scale)


def edge_kernel(visit_weight, image, mask, to_next, to_previous, ends, sems):
    last = ROWS - EDGE
    copies = [
        pltpu.make_async_copy(mask.at[pl.ds(0, EDGE)], ends.at[0], sems.at[0]),
        pltpu.make_async_copy(mask.at[pl.ds(last, EDGE)], ends.at[1], sems.at[1]),
        pltpu.make_async_copy(image.at[pl.ds(last, EDGE)], to_next.at[pl.ds(0, EDGE)], sems.at[2]),
        pltpu.make_async_copy(image.at[pl.ds(0, EDGE)], to_previous.at[pl.ds(0, EDGE)], sems.at[3]),
    ]
    for copy in copies:
        copy.start()
    scale = visit_weight[0].astype(jnp.bfloat16).astype(jnp.float32)
    for end in range(2):
        copies[end].wait()
        weight = good_weight(ends[end], scale).astype(jnp.bfloat16)
        rows = slice((end + 1) * EDGE, (end + 2) * EDGE)
        to_next[rows, :] = weight
        to_previous[rows, :] = weight
    copies[2].wait()
    copies[3].wait()


def weight_kernel(visit_weight, mask, weights, held, sems):
    copies = []
    for part in range(4):
        rows = pl.ds(part * 32, 32)
        copies.append(pltpu.make_async_copy(mask.at[rows], held.at[rows], sems.at[part]))
        copies[part].start()
    scale = visit_weight[0].astype(jnp.bfloat16).astype(jnp.float32)
    for part in range(4):
        copies[part].wait()
        rows = slice(part * 32, part * 32 + 32)
        weights[rows, :] = good_weight(held[rows, :], scale).astype(jnp.bfloat16)


def conv_kernel(tile, before, image, after, table, weights, flux, edges, stack):
    t = tile[0]
    for group in range(10):
        if group == 0:
            strip = jnp.where(t > 0, before[:EDGE, :].astype(jnp.float32), 0.0)
        elif group == 9:
            strip = jnp.where(t < NTILE - 1, after[:EDGE, :].astype(jnp.float32), 0.0)
        else:
            strip = image[(group - 1) * 16 : group * 16, :].astype(jnp.float32)
        strip = jnp.concatenate([strip, jnp.zeros((16, 128), jnp.float32)], axis=1)
        for i in range(TAPS):
            moved = strip if i == HALF else pltpu.roll(strip, (HALF - i) % (WIDTH + 128), 1)
            moved = moved[:, :WIDTH].astype(jnp.bfloat16)
            if group < 6:
                at = i * WINDOW + group * 16
                stack[0, at : at + 16, :] = moved
            if group >= 4:
                at = i * WINDOW + group * 16 - BAND
                stack[1, at : at + 16, :] = moved
    stack[:, USED:, :] = jnp.zeros((2, DEPTH - USED, WIDTH), jnp.bfloat16)
    for band in range(2):
        rows = slice(band * BAND, (band + 1) * BAND)
        for n in range(4):
            columns = slice(n * 256, (n + 1) * 256)
            parts = jnp.dot(
                table[band], stack[band, :, columns], preferred_element_type=jnp.float32
            )
            x = lax.broadcasted_iota(jnp.int32, (BAND, 256), 1) + n * 256
            xn = (2.0 * x.astype(jnp.float32) + 1.0) / WIDTH - 1.0
            conv = parts[:BAND] + xn * (parts[BAND : 2 * BAND] + xn * parts[2 * BAND :])
            flux[rows, columns] = (weights[rows, columns].astype(jnp.float32) * conv).astype(
                jnp.bfloat16
            )
    edges[:EDGE, :] = flux[:EDGE, :]
    edges[EDGE:, :] = flux[ROWS - EDGE :, :]


def warp_plane(t, own, far, after, before, row_warp, col_warp, cutout, rowed):
    for block, edges in ((lax.rem(t + 1, NTILE), after), (lax.rem(t + 3, NTILE), before)):
        start = pl.multiple_of(block * ROWS, ROWS)
        cutout[pl.ds(start + EDGE, ROWS - 2 * EDGE), :] = jnp.zeros(
            (ROWS - 2 * EDGE, WIDTH), jnp.bfloat16
        )
        cutout[pl.ds(start, EDGE), :] = edges[:EDGE, :]
        cutout[pl.ds(start + ROWS - EDGE, EDGE), :] = edges[EDGE:, :]
    cutout[pl.ds(pl.multiple_of(t * ROWS, ROWS), ROWS), :] = own[...]
    cutout[pl.ds(pl.multiple_of(lax.rem(t + 2, NTILE) * ROWS, ROWS), ROWS), :] = far[...]
    rowed[...] = jnp.dot(row_warp[...], cutout[...], preferred_element_type=jnp.float32).astype(
        jnp.bfloat16
    )
    for n in range(4):
        low, high = max(0, 256 * n - 128), min(WIDTH, 256 * n + 384)
        yield (
            n,
            jnp.dot(
                rowed[:, low:high],
                col_warp[low:high, 256 * n : 256 * n + 256],
                preferred_element_type=jnp.float32,
            ).astype(jnp.bfloat16),
        )


def warp_weight_kernel(
    tile, own, far, after, before, row_warp, col_warp, warped, cutout, rowed
):
    after, before = after.at[pl.ds(EDGE, 2 * EDGE)], before.at[pl.ds(EDGE, 2 * EDGE)]
    for n, part in warp_plane(
        tile[0], own, far, after, before, row_warp, col_warp, cutout, rowed
    ):
        warped[:, 256 * n : 256 * n + 256] = part


def warp_flux_kernel(
    tile,
    dest_slot,
    own,
    far,
    after,
    before,
    row_warp,
    col_warp,
    warped_weight,
    notes,
    outgoing,
    cutout,
    rowed,
):
    outgoing[:, 64:, :] = notes[...]
    for n, part in warp_plane(
        tile[0], own, far, after, before, row_warp, col_warp, cutout, rowed
    ):
        for down in range(8):
            for c in range(2):
                column = 2 * n + c
                slot = dest_slot[down * 8 + column]
                owner, at = slot // 2, pl.multiple_of(lax.rem(slot, 2) * 32, 32)
                rows = slice(down * 16, down * 16 + 16)
                outgoing[owner, pl.ds(at, 16), :] = part[rows, c * 128 : c * 128 + 128]
                outgoing[owner, pl.ds(at + 16, 16), :] = warped_weight[
                    rows, column * 128 : column * 128 + 128
                ]


def patch_kernel(arriving, coadd, reply, sums, served, note, table, sem):
    notes = arriving[0, 64:, :].astype(jnp.float32)
    for sender in range(1, 64):
        notes = notes + arriving[sender, 64:, :].astype(jnp.float32)
    note[...] = notes.astype(jnp.int32)
    copy = pltpu.make_async_copy(note, table, sem)
    copy.start()
    sums[...] = jnp.zeros_like(sums)
    copy.wait()

    def add(sender, _):
        for rank in range(2):
            at = table[0, 2 * sender + rank]
            sums[at] = sums[at] + arriving[sender, rank * 32 : rank * 32 + 32, :].astype(jnp.float32)
        return 0

    lax.fori_loop(0, 64, add, 0, unroll=4)
    for block in range(NBLK):
        down, c = block // 8, block % 8
        value = sums[block, :16, :] / jnp.maximum(sums[block, 16:, :], FLOOR)
        coadd[down * 16 : down * 16 + 16, c * 128 : c * 128 + 128] = value
        served[block] = value.astype(jnp.bfloat16)

    def serve(sender, _):
        for rank in range(2):
            reply[2 * sender + rank] = served[table[1, 2 * sender + rank]]
        return 0

    lax.fori_loop(0, 64, serve, 0, unroll=4)


def difference_kernel(tmpl_slot, returned, new_science, difference):
    for block in range(NBLK):
        down, c = block // 8, block % 8
        at = (slice(down * 16, down * 16 + 16), slice(c * 128, c * 128 + 128))
        difference[at] = new_science[at] - returned[tmpl_slot[block]].astype(jnp.float32)


def per_device(
    visit_image,
    mask_bits,
    visit_weight,
    basis_cols,
    basis_rows,
    kernel_coef,
    row_warp,
    col_warp,
    dest_owner,
    dest_block,
    new_science,
    tmpl_owner,
    tmpl_block,
):
    f32, bf16, i32 = jnp.float32, jnp.bfloat16, jnp.int32
    struct = jax.ShapeDtypeStruct
    tile = lax.axis_index("tile").astype(i32).reshape(1)
    home = lax.axis_index("ccd").astype(i32).reshape(1)
    up = [(i, (i + 1) % NTILE) for i in range(NTILE)]
    down = [(i, (i + 3) % NTILE) for i in range(NTILE)]
    across = [(i, (i + 2) % NTILE) for i in range(NTILE)]

    to_next, to_previous = call(
        edge_kernel,
        (struct((3 * EDGE, WIDTH), bf16),) * 2,
        [SMEM, HBM, HBM],
        (VMEM, VMEM),
        [pltpu.VMEM((2, EDGE, WIDTH), i32), pltpu.SemaphoreType.DMA((4,))],
        "edges",
        100_000,
        400_000,
    )(visit_weight, in_hbm(visit_image), in_hbm(mask_bits))
    before = lax.ppermute(to_next, "tile", up)
    after = lax.ppermute(to_previous, "tile", down)
    weights = call(
        weight_kernel,
        struct((ROWS, WIDTH), bf16),
        [SMEM, HBM],
        VMEM,
        [pltpu.VMEM((ROWS, WIDTH), i32), pltpu.SemaphoreType.DMA((4,))],
        "weights",
        400_000,
        800_000,
    )(visit_weight, in_hbm(mask_bits))
    far_weights = lax.ppermute(weights, "tile", across)

    dest_slot, tmpl_slot, notes = call(
        index_kernel,
        (struct((64,), i32), struct((64,), i32), struct((64, NOTE, 128), bf16)),
        [SMEM] * 5,
        (SMEM, SMEM, VMEM),
        [pltpu.SMEM((128,), i32), pltpu.SMEM((256,), i32)],
        "slots",
        2_000_000,
        1_000_000,
    )(home, dest_owner[:, 0], dest_block, tmpl_owner[:, 0], tmpl_block)

    taps = call(
        table_kernel,
        struct((2, 3 * BAND, DEPTH), bf16),
        [SMEM, VMEM, VMEM, VMEM],
        VMEM,
        [pltpu.VMEM((128, NB), f32)],
        "taps",
        10_000_000,
        2_000_000,
    )(tile, kernel_coef.transpose(2, 0, 1), basis_cols.T, basis_rows.T)
    flux, edges = call(
        conv_kernel,
        (struct((ROWS, WIDTH), bf16), struct((2 * EDGE, WIDTH), bf16)),
        [SMEM] + [VMEM] * 5,
        (VMEM, VMEM),
        [pltpu.VMEM((2, DEPTH, WIDTH), bf16)],
        "matching",
        2 * 2 * 192 * DEPTH * WIDTH,
        3_000_000,
    )(tile, before, visit_image, after, taps, weights)
    far_flux = lax.ppermute(flux, "tile", across)
    after_flux = lax.ppermute(edges, "tile", down)
    before_flux = lax.ppermute(edges, "tile", up)
    scratch = [pltpu.VMEM((CUTOUT, WIDTH), bf16), pltpu.VMEM((ROWS, WIDTH), bf16)]
    warped_weight = call(
        warp_weight_kernel,
        struct((ROWS, WIDTH), bf16),
        [SMEM] + [VMEM] * 6,
        VMEM,
        scratch,
        "warp_weight",
        2 * 128 * WIDTH * WIDTH,
        4_000_000,
    )(tile, weights, far_weights, after, before, row_warp, col_warp[0])
    outgoing = call(
        warp_flux_kernel,
        struct((64, MESSAGE, 128), bf16),
        [SMEM, SMEM] + [VMEM] * 8,
        VMEM,
        scratch,
        "warp_flux",
        2 * 128 * WIDTH * WIDTH,
        5_000_000,
    )(
        tile,
        dest_slot,
        flux,
        far_flux,
        after_flux,
        before_flux,
        row_warp,
        col_warp[0],
        warped_weight,
        notes,
    )
    arriving = lax.all_to_all(outgoing, "ccd", split_axis=0, concat_axis=0, tiled=True)
    coadd, reply = call(
        patch_kernel,
        (struct((ROWS, WIDTH), f32), struct((SLOTS, 16, 128), bf16)),
        [VMEM],
        (VMEM, VMEM),
        [
            pltpu.VMEM((NBLK + 8, 32, 128), f32),
            pltpu.VMEM((NBLK, 16, 128), bf16),
            pltpu.VMEM((NOTE, 128), i32),
            pltpu.SMEM((NOTE, 128), i32),
            pltpu.SemaphoreType.DMA,
        ],
        "patch",
        1_000_000,
        2_000_000,
    )(arriving)
    returned = lax.all_to_all(reply, "ccd", split_axis=0, concat_axis=0, tiled=True)
    difference = call(
        difference_kernel,
        struct((ROWS, WIDTH), f32),
        [SMEM, VMEM, VMEM],
        VMEM,
        [],
        "difference",
        1_000_000,
        2_000_000,
    )(tmpl_slot, returned, new_science)
    return coadd, difference


def solution(mesh):
    both = P(("ccd", "tile"), None)
    return jax.shard_map(
        per_device,
        mesh=mesh,
        in_specs=(
            both,
            both,
            P("ccd"),
            P(),
            P(),
            P("ccd", None, None),
            both,
            P("ccd", None, None),
            both,
            P(("ccd", "tile")),
            both,
            both,
            P(("ccd", "tile")),
        ),
        out_specs=(both, both),
        check_vma=False,
    )
```

```python
import functools

import jax
import jax.numpy as jnp
from jax import lax
from jax.experimental import pallas as pl
from jax.experimental.pallas import tpu as pltpu
from jax.sharding import PartitionSpec as P

BLOCK_ROWS = 16
BLOCK_COLUMNS = 128
FLOOR = 1.0

ROWS = 128
WIDTH = 1024
CUTOUT = 512
NTILE = 4
NB = 31
TAPS = 21
HALF = 10
EDGE = 16
BAND = 64
WINDOW = 96
DEPTH = 2048
USED = TAPS * WINDOW
NBLK = 64
SLOTS = 128
NOTE = 8
MESSAGE = 64 + NOTE

VMEM = pl.BlockSpec(memory_space=pltpu.VMEM)
ANY = pl.BlockSpec(memory_space=pl.ANY)
HBM = pl.BlockSpec(memory_space=pltpu.HBM)
SMEM = pl.BlockSpec(memory_space=pltpu.SMEM)


def in_hbm(array):
    return pltpu.with_memory_space_constraint(array, pltpu.HBM)


def call(body, out_shape, in_specs, out_specs, scratch, name, flops, nbytes):
    return pl.pallas_call(
        body,
        out_shape=out_shape,
        in_specs=in_specs,
        out_specs=out_specs,
        scratch_shapes=scratch,
        name=name,
        compiler_params=pltpu.CompilerParams(vmem_limit_bytes=20 * 1024 * 1024),
        cost_estimate=pl.CostEstimate(flops=flops, bytes_accessed=nbytes, transcendentals=0),
    )


def index_kernel(
    home,
    dest_owner,
    dest_block,
    tmpl_owner,
    tmpl_block,
    dest_slot,
    tmpl_slot,
    notes,
    count,
    table,
):
    def clear(i, _):
        count[i] = 0
        count[64 + i] = 0
        table[4 * i] = NBLK
        table[4 * i + 1] = NBLK
        table[4 * i + 2] = 0
        table[4 * i + 3] = 0
        return 0

    lax.fori_loop(0, 64, clear, 0, unroll=8)

    def place(k, _):
        owner = dest_owner[k]
        rank = count[owner]
        count[owner] = rank + 1
        dest_slot[k] = 2 * owner + rank
        table[4 * owner + rank] = dest_block[k]
        asked = tmpl_owner[k]
        rank = count[64 + asked]
        count[64 + asked] = rank + 1
        tmpl_slot[k] = 2 * asked + rank
        table[4 * asked + 2 + rank] = tmpl_block[k]
        return 0

    lax.fori_loop(0, 64, place, 0, unroll=8)

    row = lax.broadcasted_iota(jnp.int32, (NOTE, 128), 0)
    lane = lax.broadcasted_iota(jnp.int32, (NOTE, 128), 1) - 2 * home[0]
    for patch in range(64):
        note = jnp.zeros((NOTE, 128), jnp.int32)
        for kind in range(2):
            for rank in range(2):
                here = (row == kind) & (lane == rank)
                note = jnp.where(here, table[4 * patch + 2 * kind + rank], note)
        notes[patch] = note.astype(jnp.float32).astype(jnp.bfloat16)


def table_kernel(tile, coef_in, cols_in, rows_in, table, wide, coef, cols_t, rows_t, sems):
    copies = []
    for source, held in ((coef_in, coef), (cols_in, cols_t), (rows_in, rows_t)):
        copies.append(pltpu.make_async_copy(source, held, sems.at[len(copies)]))
        copies[-1].start()
    wide[...] = jnp.zeros_like(wide)
    for copy in copies:
        copy.wait()
    wide[6 : 6 + TAPS, :] = cols_t[...].astype(jnp.float32)
    taps = []
    for p in range(6):
        taps.append(
            lax.dot_general(
                rows_t[...].astype(jnp.float32) * coef[p],
                wide[...],
                (((1,), (1,)), ((), ())),
                preferred_element_type=jnp.float32,
                precision=lax.Precision.HIGHEST,
            )
        )
    lane = lax.broadcasted_iota(jnp.int32, (BAND, 128), 1)
    row = lax.broadcasted_iota(jnp.int32, (BAND, 128), 0)
    for band in range(2):
        first = tile[0] * ROWS + band * BAND
        yn = (2.0 * (first + row).astype(jnp.float32) + 1.0) / CUTOUT - 1.0
        yy = yn * yn

        def turned(i):
            v = [jnp.broadcast_to(taps[p][i : i + 1, :], (BAND, 128)) for p in range(6)]
            mixed = (v[0] + yn * v[1] + yy * v[3], v[2] + yn * v[4], v[5])
            return [
                pltpu.roll(m, (i * WINDOW) % 128, 1, stride=1, stride_axis=0) for m in mixed
            ]

        held = {}
        for column in range(DEPTH // 128):
            left = (128 * column) // WINDOW
            bound = (left + 1) * WINDOW - 128 * column
            for i in (left, left + 1):
                if i < TAPS and i not in held:
                    held[i] = turned(i)
            for q in range(3):
                other = held[left + 1][q] if left + 1 < TAPS else jnp.zeros((BAND, 128), jnp.float32)
                table[band, q * BAND : (q + 1) * BAND, column * 128 : (column + 1) * 128] = jnp.where(
                    lane < bound, held[left][q], other
                ).astype(jnp.bfloat16)
            held = {i: held[i] for i in held if i > left}


def good_weight(mask, scale):
    return jnp.where(jnp.bitwise_and(mask, 3) == 3, 0.0, scale)


def halo_kernel(image, to_next, to_previous, sems):
    copies = [
        pltpu.make_async_copy(image.at[pl.ds(ROWS - EDGE, EDGE)], to_next, sems.at[0]),
        pltpu.make_async_copy(image.at[pl.ds(0, EDGE)], to_previous, sems.at[1]),
    ]
    for copy in copies:
        copy.start()
    for copy in copies:
        copy.wait()


def weight_kernel(visit_weight, mask, weights, edges, held, sems):
    copies = []
    for part in range(4):
        rows = pl.ds(part * 32, 32)
        copies.append(pltpu.make_async_copy(mask.at[rows], held.at[rows], sems.at[part]))
        copies[part].start()
    scale = visit_weight[0].astype(jnp.bfloat16).astype(jnp.float32)
    for part in range(4):
        copies[part].wait()
        rows = slice(part * 32, part * 32 + 32)
        weights[rows, :] = good_weight(held[rows, :], scale).astype(jnp.bfloat16)
    edges[:EDGE, :] = weights[:EDGE, :]
    edges[EDGE:, :] = weights[ROWS - EDGE :, :]


def conv_kernel(tile, before, image, after, table, weights, flux, edges, stack, halo, sems):
    t = tile[0]
    copies = [
        pltpu.make_async_copy(before, halo.at[0], sems.at[0]),
        pltpu.make_async_copy(after, halo.at[1], sems.at[1]),
    ]
    for copy in copies:
        copy.start()
    for group in (1, 2, 3, 4, 5, 6, 7, 8, 0, 9):
        if group == 0:
            copies[0].wait()
            strip = jnp.where(t > 0, halo[0].astype(jnp.float32), 0.0)
        elif group == 9:
            copies[1].wait()
            strip = jnp.where(t < NTILE - 1, halo[1].astype(jnp.float32), 0.0)
        else:
            strip = image[(group - 1) * 16 : group * 16, :].astype(jnp.float32)
        strip = jnp.concatenate([strip, jnp.zeros((16, 128), jnp.float32)], axis=1)
        for i in range(TAPS):
            moved = strip if i == HALF else pltpu.roll(strip, (HALF - i) % (WIDTH + 128), 1)
            moved = moved[:, :WIDTH].astype(jnp.bfloat16)
            if group < 6:
                at = i * WINDOW + group * 16
                stack[0, at : at + 16, :] = moved
            if group >= 4:
                at = i * WINDOW + group * 16 - BAND
                stack[1, at : at + 16, :] = moved
    stack[:, USED:, :] = jnp.zeros((2, DEPTH - USED, WIDTH), jnp.bfloat16)
    for band in range(2):
        rows = slice(band * BAND, (band + 1) * BAND)
        for n in range(4):
            columns = slice(n * 256, (n + 1) * 256)
            parts = jnp.dot(
                table[band], stack[band, :, columns], preferred_element_type=jnp.float32
            )
            x = lax.broadcasted_iota(jnp.int32, (BAND, 256), 1) + n * 256
            xn = (2.0 * x.astype(jnp.float32) + 1.0) / WIDTH - 1.0
            conv = parts[:BAND] + xn * (parts[BAND : 2 * BAND] + xn * parts[2 * BAND :])
            flux[rows, columns] = (weights[rows, columns].astype(jnp.float32) * conv).astype(
                jnp.bfloat16
            )
    edges[:EDGE, :] = flux[:EDGE, :]
    edges[EDGE:, :] = flux[ROWS - EDGE :, :]


def near_columns(t, row_warp):
    def columns(block):
        return row_warp[:, pl.ds(pl.multiple_of(lax.rem(block, NTILE) * ROWS, ROWS), ROWS)]

    after, before = columns(t + 1), columns(t + 3)
    last = ROWS - EDGE
    parts = [columns(t + 2), after[:, :EDGE], after[:, last:], before[:, :EDGE], before[:, last:]]
    return columns(t), jnp.concatenate(parts, axis=1)


def gather_rest(rest, far, after, before):
    rest[:ROWS, :] = far[...]
    rest[ROWS : ROWS + 2 * EDGE, :] = after[...]
    rest[ROWS + 2 * EDGE :, :] = before[...]


def warp_columns(rowed, col_warp):
    for n in range(4):
        low, high = max(0, 256 * n - 128), min(WIDTH, 256 * n + 384)
        yield (
            n,
            jnp.dot(
                rowed[:, low:high],
                col_warp[low:high, 256 * n : 256 * n + 256],
                preferred_element_type=jnp.float32,
            ).astype(jnp.bfloat16),
        )


def warp_weight_kernel(
    tile, flux, own, far, after, before, row_warp, col_warp, warped, share, turn, rest, rowed
):
    near, turned = near_columns(tile[0], row_warp)
    share[...] = jnp.dot(near, flux[...], preferred_element_type=jnp.float32)
    turn[...] = turned
    gather_rest(rest, far, after, before)
    both = jnp.dot(near, own[...], preferred_element_type=jnp.float32) + jnp.dot(
        turned, rest[...], preferred_element_type=jnp.float32
    )
    rowed[...] = both.astype(jnp.bfloat16)
    for n, part in warp_columns(rowed, col_warp):
        warped[:, 256 * n : 256 * n + 256] = part


def warp_flux_kernel(
    dest_slot,
    share,
    turn,
    far,
    after,
    before,
    col_warp,
    warped_weight,
    notes,
    outgoing,
    rest,
    rowed,
):
    gather_rest(rest, far, after, before)
    rowed[...] = (
        share[...] + jnp.dot(turn[...], rest[...], preferred_element_type=jnp.float32)
    ).astype(jnp.bfloat16)
    outgoing[:, 64:, :] = notes[...]
    for n, part in warp_columns(rowed, col_warp):
        for down in range(8):
            for c in range(2):
                column = 2 * n + c
                slot = dest_slot[down * 8 + column]
                owner, at = slot // 2, pl.multiple_of(lax.rem(slot, 2) * 32, 32)
                rows = slice(down * 16, down * 16 + 16)
                outgoing[owner, pl.ds(at, 16), :] = part[rows, c * 128 : c * 128 + 128]
                outgoing[owner, pl.ds(at + 16, 16), :] = warped_weight[
                    rows, column * 128 : column * 128 + 128
                ]


def patch_kernel(arriving, coadd, reply, sums, values, served, note, table, sem, out_sem):
    notes = arriving[0, 64:, :].astype(jnp.float32)
    for sender in range(1, 64):
        notes = notes + arriving[sender, 64:, :].astype(jnp.float32)
    note[...] = notes.astype(jnp.int32)
    copy = pltpu.make_async_copy(note, table, sem)
    copy.start()
    sums[...] = jnp.zeros_like(sums)
    copy.wait()

    def add(sender, _):
        for rank in range(2):
            at = table[0, 2 * sender + rank]
            sums[at] = sums[at] + arriving[sender, rank * 32 : rank * 32 + 32, :].astype(jnp.float32)
        return 0

    lax.fori_loop(0, 64, add, 0, unroll=4)
    for block in range(NBLK):
        down, c = block // 8, block % 8
        value = sums[block, :16, :] / jnp.maximum(sums[block, 16:, :], FLOOR)
        values[down * 16 : down * 16 + 16, c * 128 : c * 128 + 128] = value
        served[block] = value.astype(jnp.bfloat16)
    out = pltpu.make_async_copy(values, coadd, out_sem)
    out.start()

    def serve(sender, _):
        for rank in range(2):
            reply[2 * sender + rank] = served[table[1, 2 * sender + rank]]
        return 0

    lax.fori_loop(0, 64, serve, 0, unroll=4)
    out.wait()


def difference_kernel(tmpl_slot, returned, new_science, difference, held, sems):
    copies = []
    for down in range(8):
        rows = slice(down * 16, down * 16 + 16)
        for c in range(8):
            columns = slice(c * 128, c * 128 + 128)
            template = returned[tmpl_slot[down * 8 + c]].astype(jnp.float32)
            held[rows, columns] = new_science[rows, columns] - template
        if down % 2 == 1:
            part = pl.ds(down * 16 - 16, 32)
            copies.append(
                pltpu.make_async_copy(held.at[part], difference.at[part], sems.at[down // 2])
            )
            copies[-1].start()
    for copy in copies:
        copy.wait()


def per_device(
    visit_image,
    mask_bits,
    visit_weight,
    basis_cols,
    basis_rows,
    kernel_coef,
    row_warp,
    col_warp,
    dest_owner,
    dest_block,
    new_science,
    tmpl_owner,
    tmpl_block,
):
    f32, bf16, i32 = jnp.float32, jnp.bfloat16, jnp.int32
    struct = jax.ShapeDtypeStruct
    tile = lax.axis_index("tile").astype(i32).reshape(1)
    home = lax.axis_index("ccd").astype(i32).reshape(1)
    up = [(i, (i + 1) % NTILE) for i in range(NTILE)]
    down = [(i, (i + 3) % NTILE) for i in range(NTILE)]
    across = [(i, (i + 2) % NTILE) for i in range(NTILE)]

    to_next, to_previous = call(
        halo_kernel,
        (struct((EDGE, WIDTH), bf16),) * 2,
        [HBM],
        (VMEM, VMEM),
        [pltpu.SemaphoreType.DMA((2,))],
        "halo",
        1000,
        100_000,
    )(in_hbm(visit_image))
    before = lax.ppermute(to_next, "tile", up)
    after = lax.ppermute(to_previous, "tile", down)
    weights, weight_edges = call(
        weight_kernel,
        (struct((ROWS, WIDTH), bf16), struct((2 * EDGE, WIDTH), bf16)),
        [SMEM, HBM],
        (VMEM, VMEM),
        [pltpu.VMEM((ROWS, WIDTH), i32), pltpu.SemaphoreType.DMA((4,))],
        "weights",
        400_000,
        800_000,
    )(visit_weight, in_hbm(mask_bits))
    before_weights = lax.ppermute(weight_edges, "tile", up)
    after_weights = lax.ppermute(weight_edges, "tile", down)
    far_weights = lax.ppermute(weights, "tile", across)

    dest_slot, tmpl_slot, notes = call(
        index_kernel,
        (struct((64,), i32), struct((64,), i32), struct((64, NOTE, 128), bf16)),
        [SMEM] * 5,
        (SMEM, SMEM, VMEM),
        [pltpu.SMEM((128,), i32), pltpu.SMEM((256,), i32)],
        "slots",
        2_000_000,
        1_000_000,
    )(home, dest_owner[:, 0], dest_block, tmpl_owner[:, 0], tmpl_block)

    taps = call(
        table_kernel,
        struct((2, 3 * BAND, DEPTH), bf16),
        [SMEM, HBM, HBM, HBM],
        VMEM,
        [
            pltpu.VMEM((128, NB), f32),
            pltpu.VMEM((6, 1, NB), f32),
            pltpu.VMEM((TAPS, NB), bf16),
            pltpu.VMEM((TAPS, NB), bf16),
            pltpu.SemaphoreType.DMA((3,)),
        ],
        "taps",
        10_000_000,
        2_000_000,
    )(tile, in_hbm(kernel_coef.transpose(2, 0, 1)), in_hbm(basis_cols.T), in_hbm(basis_rows.T))
    flux, edges = call(
        conv_kernel,
        (struct((ROWS, WIDTH), bf16), struct((2 * EDGE, WIDTH), bf16)),
        [SMEM, ANY, VMEM, ANY, VMEM, VMEM],
        (VMEM, VMEM),
        [
            pltpu.VMEM((2, DEPTH, WIDTH), bf16),
            pltpu.VMEM((2, EDGE, WIDTH), bf16),
            pltpu.SemaphoreType.DMA((2,)),
        ],
        "matching",
        2 * 2 * 192 * DEPTH * WIDTH,
        3_000_000,
    )(tile, before, visit_image, in_hbm(after), taps, weights)
    flux, edges, before_weights, after_weights = lax.optimization_barrier(
        (flux, edges, before_weights, after_weights)
    )
    far_flux = lax.ppermute(flux, "tile", across)
    after_flux = lax.ppermute(edges, "tile", down)
    before_flux = lax.ppermute(edges, "tile", up)
    reach = ROWS + 4 * EDGE
    scratch = [pltpu.VMEM((reach, WIDTH), bf16), pltpu.VMEM((ROWS, WIDTH), bf16)]
    warped_weight, share, turn = call(
        warp_weight_kernel,
        (struct((ROWS, WIDTH), bf16), struct((ROWS, WIDTH), f32), struct((ROWS, reach), bf16)),
        [SMEM] + [VMEM] * 7,
        (VMEM,) * 3,
        scratch,
        "warp_weight",
        2 * 128 * WIDTH * WIDTH,
        4_000_000,
    )(tile, flux, weights, far_weights, after_weights, before_weights, row_warp, col_warp[0])
    outgoing = call(
        warp_flux_kernel,
        struct((64, MESSAGE, 128), bf16),
        [SMEM] + [VMEM] * 8,
        VMEM,
        scratch,
        "warp_flux",
        2 * 128 * WIDTH * WIDTH,
        5_000_000,
    )(
        dest_slot,
        share,
        turn,
        far_flux,
        after_flux,
        before_flux,
        col_warp[0],
        warped_weight,
        notes,
    )
    arriving = lax.all_to_all(outgoing, "ccd", split_axis=0, concat_axis=0, tiled=True)
    coadd, reply = call(
        patch_kernel,
        (struct((ROWS, WIDTH), f32), struct((SLOTS, 16, 128), bf16)),
        [VMEM],
        (HBM, VMEM),
        [
            pltpu.VMEM((NBLK + 8, 32, 128), f32),
            pltpu.VMEM((ROWS, WIDTH), f32),
            pltpu.VMEM((NBLK, 16, 128), bf16),
            pltpu.VMEM((NOTE, 128), i32),
            pltpu.SMEM((NOTE, 128), i32),
            pltpu.SemaphoreType.DMA,
            pltpu.SemaphoreType.DMA,
        ],
        "patch",
        1_000_000,
        2_000_000,
    )(arriving)
    returned = lax.all_to_all(reply, "ccd", split_axis=0, concat_axis=0, tiled=True)
    difference = call(
        difference_kernel,
        struct((ROWS, WIDTH), f32),
        [SMEM, VMEM, VMEM],
        HBM,
        [pltpu.VMEM((ROWS, WIDTH), f32), pltpu.SemaphoreType.DMA((4,))],
        "difference",
        1_000_000,
        2_000_000,
    )(tmpl_slot, returned, new_science)
    return coadd, difference


def solution(mesh):
    both = P(("ccd", "tile"), None)
    return jax.shard_map(
        per_device,
        mesh=mesh,
        in_specs=(
            both,
            both,
            P("ccd"),
            P(),
            P(),
            P("ccd", None, None),
            both,
            P("ccd", None, None),
            both,
            P(("ccd", "tile")),
            both,
            both,
            P(("ccd", "tile")),
        ),
        out_specs=(both, both),
        check_vma=False,
    )
```

```python
import functools

import jax
import jax.numpy as jnp
from jax import lax
from jax.experimental import pallas as pl
from jax.experimental.pallas import tpu as pltpu
from jax.sharding import PartitionSpec as P

BLOCK_ROWS = 16
BLOCK_COLUMNS = 128
FLOOR = 1.0

ROWS = 128
WIDTH = 1024
CUTOUT = 512
NTILE = 4
NB = 31
TAPS = 21
HALF = 10
EDGE = 16
BAND = 64
WINDOW = 96
DEPTH = 2048
USED = TAPS * WINDOW
NBLK = 64
SLOTS = 128
NOTE = 8
MESSAGE = 64 + NOTE

VMEM = pl.BlockSpec(memory_space=pltpu.VMEM)
HBM = pl.BlockSpec(memory_space=pltpu.HBM)
SMEM = pl.BlockSpec(memory_space=pltpu.SMEM)


def in_hbm(array):
    return pltpu.with_memory_space_constraint(array, pltpu.HBM)


def call(body, out_shape, in_specs, out_specs, scratch, name, flops, nbytes):
    return pl.pallas_call(
        body,
        out_shape=out_shape,
        in_specs=in_specs,
        out_specs=out_specs,
        scratch_shapes=scratch,
        name=name,
        compiler_params=pltpu.CompilerParams(vmem_limit_bytes=20 * 1024 * 1024),
        cost_estimate=pl.CostEstimate(flops=flops, bytes_accessed=nbytes, transcendentals=0),
    )


def index_kernel(
    home,
    dest_owner,
    dest_block,
    tmpl_owner,
    tmpl_block,
    dest_slot,
    tmpl_slot,
    notes,
    count,
    table,
):
    def clear(i, _):
        count[i] = 0
        count[64 + i] = 0
        table[4 * i] = NBLK
        table[4 * i + 1] = NBLK
        table[4 * i + 2] = 0
        table[4 * i + 3] = 0
        return 0

    lax.fori_loop(0, 64, clear, 0, unroll=8)

    def place(k, _):
        owner = dest_owner[k]
        rank = count[owner]
        count[owner] = rank + 1
        dest_slot[k] = 2 * owner + rank
        table[4 * owner + rank] = dest_block[k]
        asked = tmpl_owner[k]
        rank = count[64 + asked]
        count[64 + asked] = rank + 1
        tmpl_slot[k] = 2 * asked + rank
        table[4 * asked + 2 + rank] = tmpl_block[k]
        return 0

    lax.fori_loop(0, 64, place, 0, unroll=8)

    row = lax.broadcasted_iota(jnp.int32, (NOTE, 128), 0)
    lane = lax.broadcasted_iota(jnp.int32, (NOTE, 128), 1) - 2 * home[0]
    for patch in range(64):
        note = jnp.zeros((NOTE, 128), jnp.int32)
        for kind in range(2):
            for rank in range(2):
                here = (row == kind) & (lane == rank)
                note = jnp.where(here, table[4 * patch + 2 * kind + rank], note)
        notes[patch] = note.astype(jnp.float32).astype(jnp.bfloat16)


def table_kernel(tile, coef, cols_t, rows_t, table, wide):
    wide[...] = jnp.zeros_like(wide)
    wide[6 : 6 + TAPS, :] = cols_t[...].astype(jnp.float32)
    taps = []
    for p in range(6):
        taps.append(
            lax.dot_general(
                rows_t[...].astype(jnp.float32) * coef[p],
                wide[...],
                (((1,), (1,)), ((), ())),
                preferred_element_type=jnp.float32,
                precision=lax.Precision.HIGHEST,
            )
        )
    lane = lax.broadcasted_iota(jnp.int32, (BAND, 128), 1)
    row = lax.broadcasted_iota(jnp.int32, (BAND, 128), 0)
    for band in range(2):
        first = tile[0] * ROWS + band * BAND
        yn = (2.0 * (first + row).astype(jnp.float32) + 1.0) / CUTOUT - 1.0
        yy = yn * yn

        def turned(i):
            v = [jnp.broadcast_to(taps[p][i : i + 1, :], (BAND, 128)) for p in range(6)]
            mixed = (v[0] + yn * v[1] + yy * v[3], v[2] + yn * v[4], v[5])
            return [
                pltpu.roll(m, (i * WINDOW) % 128, 1, stride=1, stride_axis=0) for m in mixed
            ]

        held = {}
        for column in range(DEPTH // 128):
            left = (128 * column) // WINDOW
            bound = (left + 1) * WINDOW - 128 * column
            for i in (left, left + 1):
                if i < TAPS and i not in held:
                    held[i] = turned(i)
            for q in range(3):
                other = held[left + 1][q] if left + 1 < TAPS else jnp.zeros((BAND, 128), jnp.float32)
                table[band, q * BAND : (q + 1) * BAND, column * 128 : (column + 1) * 128] = jnp.where(
                    lane < bound, held[left][q], other
                ).astype(jnp.bfloat16)
            held = {i: held[i] for i in held if i > left}


def edge_kernel(
    image, mask, coef, cols, rows, to_next, to_previous, good, coef_near, cols_near, rows_near, held, sems
):
    last = ROWS - EDGE
    copies = []
    parts = [(0, EDGE), (last, EDGE)] + [(EDGE + 32 * part, 32) for part in range(3)]
    for first, count in parts[:2]:
        span = pl.ds(first, count)
        copies.append(pltpu.make_async_copy(mask.at[span], held.at[span], sems.at[len(copies)]))
    copies.append(
        pltpu.make_async_copy(image.at[pl.ds(last, EDGE)], to_next.at[pl.ds(0, EDGE)], sems.at[2])
    )
    copies.append(
        pltpu.make_async_copy(image.at[pl.ds(0, EDGE)], to_previous.at[pl.ds(0, EDGE)], sems.at[3])
    )
    for first, count in parts[2:]:
        span = pl.ds(first, count)
        copies.append(pltpu.make_async_copy(mask.at[span], held.at[span], sems.at[len(copies)]))
    for source, near in ((coef, coef_near), (cols, cols_near), (rows, rows_near)):
        copies.append(pltpu.make_async_copy(source, near, sems.at[len(copies)]))
    for copy in copies:
        copy.start()
    for (first, count), copy in zip(parts, copies[:2] + copies[4:7]):
        copy.wait()
        span = slice(first, first + count)
        flags = jnp.where(jnp.bitwise_and(held[span, :], 3) == 3, 0.0, 1.0).astype(jnp.bfloat16)
        good[span, :] = flags
        if count == EDGE:
            at = slice(EDGE, 2 * EDGE) if first == 0 else slice(2 * EDGE, 3 * EDGE)
            to_next[at, :] = flags
            to_previous[at, :] = flags
    for copy in copies[2:4] + copies[7:]:
        copy.wait()


def conv_kernel(tile, visit_weight, before, image, after, table, good, flux, edges, stack):
    t = tile[0]
    for group in range(10):
        if group == 0:
            strip = jnp.where(t > 0, before[:EDGE, :].astype(jnp.float32), 0.0)
        elif group == 9:
            strip = jnp.where(t < NTILE - 1, after[:EDGE, :].astype(jnp.float32), 0.0)
        else:
            strip = image[(group - 1) * 16 : group * 16, :].astype(jnp.float32)
        strip = jnp.concatenate([strip, jnp.zeros((16, 128), jnp.float32)], axis=1)
        for i in range(TAPS):
            moved = strip if i == HALF else pltpu.roll(strip, (HALF - i) % (WIDTH + 128), 1)
            moved = moved[:, :WIDTH].astype(jnp.bfloat16)
            if group < 6:
                at = i * WINDOW + group * 16
                stack[0, at : at + 16, :] = moved
            if group >= 4:
                at = i * WINDOW + group * 16 - BAND
                stack[1, at : at + 16, :] = moved
    stack[:, USED:, :] = jnp.zeros((2, DEPTH - USED, WIDTH), jnp.bfloat16)
    scale = visit_weight[0].astype(jnp.bfloat16).astype(jnp.float32)
    for band in range(2):
        rows = slice(band * BAND, (band + 1) * BAND)
        for n in range(4):
            columns = slice(n * 256, (n + 1) * 256)
            parts = jnp.dot(
                table[band], stack[band, :, columns], preferred_element_type=jnp.float32
            )
            x = lax.broadcasted_iota(jnp.int32, (BAND, 256), 1) + n * 256
            xn = (2.0 * x.astype(jnp.float32) + 1.0) / WIDTH - 1.0
            conv = parts[:BAND] + xn * (parts[BAND : 2 * BAND] + xn * parts[2 * BAND :])
            weight = scale * good[rows, columns].astype(jnp.float32)
            flux[rows, columns] = (weight * conv).astype(jnp.bfloat16)
    edges[:EDGE, :] = flux[:EDGE, :]
    edges[EDGE:, :] = flux[ROWS - EDGE :, :]


def near_columns(t, row_warp):
    def columns(block):
        return row_warp[:, pl.ds(pl.multiple_of(lax.rem(block, NTILE) * ROWS, ROWS), ROWS)]

    after, before = columns(t + 1), columns(t + 3)
    last = ROWS - EDGE
    parts = [columns(t + 2), after[:, :EDGE], after[:, last:], before[:, :EDGE], before[:, last:]]
    return columns(t), jnp.concatenate(parts, axis=1)


def gather_rest(rest, far, after, before):
    rest[:ROWS, :] = far[...]
    rest[ROWS : ROWS + 2 * EDGE, :] = after[...]
    rest[ROWS + 2 * EDGE :, :] = before[...]


def warp_columns(rowed, col_warp):
    for n in range(4):
        low, high = max(0, 256 * n - 128), min(WIDTH, 256 * n + 384)
        yield (
            n,
            jnp.dot(
                rowed[:, low:high],
                col_warp[low:high, 256 * n : 256 * n + 256],
                preferred_element_type=jnp.float32,
            ).astype(jnp.bfloat16),
        )


def warp_weight_kernel(
    tile,
    visit_weight,
    flux,
    own,
    far,
    after,
    before,
    row_warp,
    col_warp,
    warped,
    share,
    turn,
    rest,
    rowed,
):
    near, turned = near_columns(tile[0], row_warp)
    share[...] = jnp.dot(near, flux[...], preferred_element_type=jnp.float32)
    turn[...] = turned
    gather_rest(rest, far, after.at[pl.ds(EDGE, 2 * EDGE)], before.at[pl.ds(EDGE, 2 * EDGE)])
    both = jnp.dot(near, own[...], preferred_element_type=jnp.float32) + jnp.dot(
        turned, rest[...], preferred_element_type=jnp.float32
    )
    scale = visit_weight[0].astype(jnp.bfloat16).astype(jnp.float32)
    rowed[...] = (scale * both).astype(jnp.bfloat16)
    for n, part in warp_columns(rowed, col_warp):
        warped[:, 256 * n : 256 * n + 256] = part


def warp_flux_kernel(
    dest_slot,
    share,
    turn,
    far,
    after,
    before,
    col_warp,
    warped_weight,
    notes,
    outgoing,
    rest,
    rowed,
):
    gather_rest(rest, far, after, before)
    rowed[...] = (
        share[...] + jnp.dot(turn[...], rest[...], preferred_element_type=jnp.float32)
    ).astype(jnp.bfloat16)
    outgoing[:, 64:, :] = notes[...]
    for n, part in warp_columns(rowed, col_warp):
        for down in range(8):
            for c in range(2):
                column = 2 * n + c
                slot = dest_slot[down * 8 + column]
                owner, at = slot // 2, pl.multiple_of(lax.rem(slot, 2) * 32, 32)
                rows = slice(down * 16, down * 16 + 16)
                outgoing[owner, pl.ds(at, 16), :] = part[rows, c * 128 : c * 128 + 128]
                outgoing[owner, pl.ds(at + 16, 16), :] = warped_weight[
                    rows, column * 128 : column * 128 + 128
                ]


def patch_kernel(arriving, coadd, reply, sums, values, served, note, table, sem, out_sem):
    notes = arriving[0, 64:, :].astype(jnp.float32)
    for sender in range(1, 64):
        notes = notes + arriving[sender, 64:, :].astype(jnp.float32)
    note[...] = notes.astype(jnp.int32)
    copy = pltpu.make_async_copy(note, table, sem)
    copy.start()
    sums[...] = jnp.zeros_like(sums)
    copy.wait()

    def add(sender, _):
        for rank in range(2):
            at = table[0, 2 * sender + rank]
            sums[at] = sums[at] + arriving[sender, rank * 32 : rank * 32 + 32, :].astype(jnp.float32)
        return 0

    lax.fori_loop(0, 64, add, 0, unroll=4)
    for block in range(NBLK):
        down, c = block // 8, block % 8
        value = sums[block, :16, :] / jnp.maximum(sums[block, 16:, :], FLOOR)
        values[down * 16 : down * 16 + 16, c * 128 : c * 128 + 128] = value
        served[block] = value.astype(jnp.bfloat16)
    out = pltpu.make_async_copy(values, coadd, out_sem)
    out.start()

    def serve(sender, _):
        for rank in range(2):
            reply[2 * sender + rank] = served[table[1, 2 * sender + rank]]
        return 0

    lax.fori_loop(0, 64, serve, 0, unroll=4)
    out.wait()


def difference_kernel(tmpl_slot, returned, new_science, difference, held, sems):
    copies = []
    for down in range(8):
        rows = slice(down * 16, down * 16 + 16)
        for c in range(8):
            columns = slice(c * 128, c * 128 + 128)
            template = returned[tmpl_slot[down * 8 + c]].astype(jnp.float32)
            held[rows, columns] = new_science[rows, columns] - template
        if down % 2 == 1:
            part = pl.ds(down * 16 - 16, 32)
            copies.append(
                pltpu.make_async_copy(held.at[part], difference.at[part], sems.at[down // 2])
            )
            copies[-1].start()
    for copy in copies:
        copy.wait()


def per_device(
    visit_image,
    mask_bits,
    visit_weight,
    basis_cols,
    basis_rows,
    kernel_coef,
    row_warp,
    col_warp,
    dest_owner,
    dest_block,
    new_science,
    tmpl_owner,
    tmpl_block,
):
    f32, bf16, i32 = jnp.float32, jnp.bfloat16, jnp.int32
    struct = jax.ShapeDtypeStruct
    tile = lax.axis_index("tile").astype(i32).reshape(1)
    home = lax.axis_index("ccd").astype(i32).reshape(1)
    up = [(i, (i + 1) % NTILE) for i in range(NTILE)]
    down = [(i, (i + 3) % NTILE) for i in range(NTILE)]
    across = [(i, (i + 2) % NTILE) for i in range(NTILE)]

    to_next, to_previous, good, coef, cols_t, rows_t = call(
        edge_kernel,
        (
            struct((3 * EDGE, WIDTH), bf16),
            struct((3 * EDGE, WIDTH), bf16),
            struct((ROWS, WIDTH), bf16),
            struct((6, 1, NB), f32),
            struct((TAPS, NB), bf16),
            struct((TAPS, NB), bf16),
        ),
        [HBM] * 5,
        (VMEM,) * 6,
        [pltpu.VMEM((ROWS, WIDTH), i32), pltpu.SemaphoreType.DMA((10,))],
        "edges",
        400_000,
        1_000_000,
    )(
        in_hbm(visit_image),
        in_hbm(mask_bits),
        in_hbm(kernel_coef.transpose(2, 0, 1)),
        in_hbm(basis_cols.T),
        in_hbm(basis_rows.T),
    )
    before = lax.ppermute(to_next, "tile", up)
    after = lax.ppermute(to_previous, "tile", down)
    far_good = lax.ppermute(good, "tile", across)

    dest_slot, tmpl_slot, notes = call(
        index_kernel,
        (struct((64,), i32), struct((64,), i32), struct((64, NOTE, 128), bf16)),
        [SMEM] * 5,
        (SMEM, SMEM, VMEM),
        [pltpu.SMEM((128,), i32), pltpu.SMEM((256,), i32)],
        "slots",
        2_000_000,
        1_000_000,
    )(home, dest_owner[:, 0], dest_block, tmpl_owner[:, 0], tmpl_block)

    taps = call(
        table_kernel,
        struct((2, 3 * BAND, DEPTH), bf16),
        [SMEM, VMEM, VMEM, VMEM],
        VMEM,
        [pltpu.VMEM((128, NB), f32)],
        "taps",
        10_000_000,
        2_000_000,
    )(tile, coef, cols_t, rows_t)
    flux, edges = call(
        conv_kernel,
        (struct((ROWS, WIDTH), bf16), struct((2 * EDGE, WIDTH), bf16)),
        [SMEM, SMEM] + [VMEM] * 5,
        (VMEM, VMEM),
        [pltpu.VMEM((2, DEPTH, WIDTH), bf16)],
        "matching",
        2 * 2 * 192 * DEPTH * WIDTH,
        3_000_000,
    )(tile, visit_weight, before, visit_image, after, taps, good)
    far_flux = lax.ppermute(flux, "tile", across)
    after_flux = lax.ppermute(edges, "tile", down)
    before_flux = lax.ppermute(edges, "tile", up)
    reach = ROWS + 4 * EDGE
    scratch = [pltpu.VMEM((reach, WIDTH), bf16), pltpu.VMEM((ROWS, WIDTH), bf16)]
    warped_weight, share, turn = call(
        warp_weight_kernel,
        (struct((ROWS, WIDTH), bf16), struct((ROWS, WIDTH), f32), struct((ROWS, reach), bf16)),
        [SMEM, SMEM] + [VMEM] * 7,
        (VMEM,) * 3,
        scratch,
        "warp_weight",
        2 * 128 * WIDTH * WIDTH,
        4_000_000,
    )(tile, visit_weight, flux, good, far_good, after, before, row_warp, col_warp[0])
    outgoing = call(
        warp_flux_kernel,
        struct((64, MESSAGE, 128), bf16),
        [SMEM] + [VMEM] * 8,
        VMEM,
        scratch,
        "warp_flux",
        2 * 128 * WIDTH * WIDTH,
        5_000_000,
    )(
        dest_slot,
        share,
        turn,
        far_flux,
        after_flux,
        before_flux,
        col_warp[0],
        warped_weight,
        notes,
    )
    arriving = lax.all_to_all(outgoing, "ccd", split_axis=0, concat_axis=0, tiled=True)
    coadd, reply = call(
        patch_kernel,
        (struct((ROWS, WIDTH), f32), struct((SLOTS, 16, 128), bf16)),
        [VMEM],
        (HBM, VMEM),
        [
            pltpu.VMEM((NBLK + 8, 32, 128), f32),
            pltpu.VMEM((ROWS, WIDTH), f32),
            pltpu.VMEM((NBLK, 16, 128), bf16),
            pltpu.VMEM((NOTE, 128), i32),
            pltpu.SMEM((NOTE, 128), i32),
            pltpu.SemaphoreType.DMA,
            pltpu.SemaphoreType.DMA,
        ],
        "patch",
        1_000_000,
        2_000_000,
    )(arriving)
    returned = lax.all_to_all(reply, "ccd", split_axis=0, concat_axis=0, tiled=True)
    difference = call(
        difference_kernel,
        struct((ROWS, WIDTH), f32),
        [SMEM, VMEM, VMEM],
        HBM,
        [pltpu.VMEM((ROWS, WIDTH), f32), pltpu.SemaphoreType.DMA((4,))],
        "difference",
        1_000_000,
        2_000_000,
    )(tmpl_slot, returned, new_science)
    return coadd, difference


def solution(mesh):
    both = P(("ccd", "tile"), None)
    return jax.shard_map(
        per_device,
        mesh=mesh,
        in_specs=(
            both,
            both,
            P("ccd"),
            P(),
            P(),
            P("ccd", None, None),
            both,
            P("ccd", None, None),
            both,
            P(("ccd", "tile")),
            both,
            both,
            P(("ccd", "tile")),
        ),
        out_specs=(both, both),
        check_vma=False,
    )
```

```python
import functools

import jax
import jax.numpy as jnp
from jax import lax
from jax.experimental import pallas as pl
from jax.experimental.pallas import tpu as pltpu
from jax.sharding import PartitionSpec as P

BLOCK_ROWS = 16
BLOCK_COLUMNS = 128
FLOOR = 1.0

ROWS = 128
WIDTH = 1024
CUTOUT = 512
NTILE = 4
NB = 31
TAPS = 21
HALF = 10
EDGE = 16
BAND = 64
WINDOW = 96
DEPTH = 2048
USED = TAPS * WINDOW
NBLK = 64
SLOTS = 128
NOTE = 8
MESSAGE = 64 + NOTE

VMEM = pl.BlockSpec(memory_space=pltpu.VMEM)
HBM = pl.BlockSpec(memory_space=pltpu.HBM)
SMEM = pl.BlockSpec(memory_space=pltpu.SMEM)


def in_hbm(array):
    return pltpu.with_memory_space_constraint(array, pltpu.HBM)


def call(body, out_shape, in_specs, out_specs, scratch, name, flops, nbytes):
    return pl.pallas_call(
        body,
        out_shape=out_shape,
        in_specs=in_specs,
        out_specs=out_specs,
        scratch_shapes=scratch,
        name=name,
        compiler_params=pltpu.CompilerParams(vmem_limit_bytes=20 * 1024 * 1024),
        cost_estimate=pl.CostEstimate(flops=flops, bytes_accessed=nbytes, transcendentals=0),
    )


def index_kernel(
    home,
    dest_owner,
    dest_block,
    tmpl_owner,
    tmpl_block,
    dest_slot,
    tmpl_slot,
    notes,
    count,
    table,
):
    def clear(i, _):
        count[i] = 0
        count[64 + i] = 0
        table[4 * i] = NBLK
        table[4 * i + 1] = NBLK
        table[4 * i + 2] = 0
        table[4 * i + 3] = 0
        return 0

    lax.fori_loop(0, 64, clear, 0, unroll=8)

    def place(k, _):
        owner = dest_owner[k]
        rank = count[owner]
        count[owner] = rank + 1
        dest_slot[k] = 2 * owner + rank
        table[4 * owner + rank] = dest_block[k]
        asked = tmpl_owner[k]
        rank = count[64 + asked]
        count[64 + asked] = rank + 1
        tmpl_slot[k] = 2 * asked + rank
        table[4 * asked + 2 + rank] = tmpl_block[k]
        return 0

    lax.fori_loop(0, 64, place, 0, unroll=8)

    row = lax.broadcasted_iota(jnp.int32, (NOTE, 128), 0)
    lane = lax.broadcasted_iota(jnp.int32, (NOTE, 128), 1) - 2 * home[0]
    for patch in range(64):
        note = jnp.zeros((NOTE, 128), jnp.int32)
        for kind in range(2):
            for rank in range(2):
                here = (row == kind) & (lane == rank)
                note = jnp.where(here, table[4 * patch + 2 * kind + rank], note)
        notes[patch] = note.astype(jnp.float32).astype(jnp.bfloat16)


def table_kernel(tile, coef, cols_t, rows_t, table, wide):
    wide[...] = jnp.zeros_like(wide)
    wide[6 : 6 + TAPS, :] = cols_t[...].astype(jnp.float32)
    taps = []
    for p in range(6):
        taps.append(
            lax.dot_general(
                rows_t[...].astype(jnp.float32) * coef[p],
                wide[...],
                (((1,), (1,)), ((), ())),
                preferred_element_type=jnp.float32,
                precision=lax.Precision.HIGHEST,
            )
        )
    lane = lax.broadcasted_iota(jnp.int32, (BAND, 128), 1)
    row = lax.broadcasted_iota(jnp.int32, (BAND, 128), 0)
    for band in range(2):
        first = tile[0] * ROWS + band * BAND
        yn = (2.0 * (first + row).astype(jnp.float32) + 1.0) / CUTOUT - 1.0
        yy = yn * yn

        def turned(i):
            v = [jnp.broadcast_to(taps[p][i : i + 1, :], (BAND, 128)) for p in range(6)]
            mixed = (v[0] + yn * v[1] + yy * v[3], v[2] + yn * v[4], v[5])
            return [
                pltpu.roll(m, (i * WINDOW) % 128, 1, stride=1, stride_axis=0) for m in mixed
            ]

        held = {}
        for column in range(DEPTH // 128):
            left = (128 * column) // WINDOW
            bound = (left + 1) * WINDOW - 128 * column
            for i in (left, left + 1):
                if i < TAPS and i not in held:
                    held[i] = turned(i)
            for q in range(3):
                other = held[left + 1][q] if left + 1 < TAPS else jnp.zeros((BAND, 128), jnp.float32)
                table[band, q * BAND : (q + 1) * BAND, column * 128 : (column + 1) * 128] = jnp.where(
                    lane < bound, held[left][q], other
                ).astype(jnp.bfloat16)
            held = {i: held[i] for i in held if i > left}


def edge_kernel(
    tile,
    image,
    mask,
    row_warp,
    coef,
    cols,
    rows,
    to_next,
    to_previous,
    good,
    coef_near,
    cols_near,
    rows_near,
    level,
    held,
    own_part,
    sems,
):
    last = ROWS - EDGE
    copies = []
    parts = [(0, EDGE), (last, EDGE)] + [(EDGE + 32 * part, 32) for part in range(3)]
    for first, count in parts[:2]:
        span = pl.ds(first, count)
        copies.append(pltpu.make_async_copy(mask.at[span], held.at[span], sems.at[len(copies)]))
    copies.append(
        pltpu.make_async_copy(image.at[pl.ds(last, EDGE)], to_next.at[pl.ds(0, EDGE)], sems.at[2])
    )
    copies.append(
        pltpu.make_async_copy(image.at[pl.ds(0, EDGE)], to_previous.at[pl.ds(0, EDGE)], sems.at[3])
    )
    for first, count in parts[2:]:
        span = pl.ds(first, count)
        copies.append(pltpu.make_async_copy(mask.at[span], held.at[span], sems.at[len(copies)]))
    own_columns = pl.ds(pl.multiple_of(tile[0] * ROWS, ROWS), ROWS)
    for source, near in (
        (row_warp.at[:, own_columns], own_part),
        (coef, coef_near),
        (cols, cols_near),
        (rows, rows_near),
    ):
        copies.append(pltpu.make_async_copy(source, near, sems.at[len(copies)]))
    for copy in copies:
        copy.start()
    for (first, count), copy in zip(parts, copies[:2] + copies[4:7]):
        copy.wait()
        span = slice(first, first + count)
        flags = jnp.where(jnp.bitwise_and(held[span, :], 3) == 3, 0.0, 1.0)
        good[span, :] = flags.astype(jnp.bfloat16)
    for copy in copies[2:4] + copies[7:]:
        copy.wait()
    is_level = jnp.max(jnp.abs(own_part[...].astype(jnp.float32))) > 0.0
    for i in range(8):
        level[i] = is_level.astype(jnp.int32)
    send_ends(is_level, good, to_next.at[pl.ds(EDGE, EDGE)], to_previous.at[pl.ds(EDGE, EDGE)])


def send_ends(is_level, plane, to_next, to_previous):
    head, tail = plane[:EDGE, :].astype(jnp.float32), plane[ROWS - EDGE :, :].astype(jnp.float32)
    to_next[...] = jnp.where(is_level, tail, head).astype(jnp.bfloat16)
    to_previous[...] = jnp.where(is_level, head, tail).astype(jnp.bfloat16)


def conv_kernel(
    tile, level, visit_weight, before, image, after, table, good, flux, to_next, to_previous, stack
):
    t = tile[0]
    for group in range(10):
        if group == 0:
            strip = jnp.where(t > 0, before[:EDGE, :].astype(jnp.float32), 0.0)
        elif group == 9:
            strip = jnp.where(t < NTILE - 1, after[:EDGE, :].astype(jnp.float32), 0.0)
        else:
            strip = image[(group - 1) * 16 : group * 16, :].astype(jnp.float32)
        strip = jnp.concatenate([strip, jnp.zeros((16, 128), jnp.float32)], axis=1)
        for i in range(TAPS):
            moved = strip if i == HALF else pltpu.roll(strip, (HALF - i) % (WIDTH + 128), 1)
            moved = moved[:, :WIDTH].astype(jnp.bfloat16)
            if group < 6:
                at = i * WINDOW + group * 16
                stack[0, at : at + 16, :] = moved
            if group >= 4:
                at = i * WINDOW + group * 16 - BAND
                stack[1, at : at + 16, :] = moved
    stack[:, USED:, :] = jnp.zeros((2, DEPTH - USED, WIDTH), jnp.bfloat16)
    scale = visit_weight[0].astype(jnp.bfloat16).astype(jnp.float32)
    for band in range(2):
        rows = slice(band * BAND, (band + 1) * BAND)
        for n in range(4):
            columns = slice(n * 256, (n + 1) * 256)
            parts = jnp.dot(
                table[band], stack[band, :, columns], preferred_element_type=jnp.float32
            )
            x = lax.broadcasted_iota(jnp.int32, (BAND, 256), 1) + n * 256
            xn = (2.0 * x.astype(jnp.float32) + 1.0) / WIDTH - 1.0
            conv = parts[:BAND] + xn * (parts[BAND : 2 * BAND] + xn * parts[2 * BAND :])
            weight = scale * good[rows, columns].astype(jnp.float32)
            flux[rows, columns] = (weight * conv).astype(jnp.bfloat16)
    send_ends(level[0] == 1, flux, to_next, to_previous)


def near_columns(t, is_level, row_warp):
    def columns(block):
        return row_warp[:, pl.ds(pl.multiple_of(lax.rem(block, NTILE) * ROWS, ROWS), ROWS)]

    def end(block, first_if_level):
        part = columns(block).astype(jnp.float32)
        first, last = part[:, :EDGE], part[:, ROWS - EDGE :]
        return jnp.where(is_level == first_if_level, first, last).astype(jnp.bfloat16)

    parts = [columns(t + 2), end(t + 1, True), end(t + 3, False)]
    return columns(t), jnp.concatenate(parts, axis=1)


def gather_rest(rest, far, after, before):
    rest[:ROWS, :] = far[...]
    rest[ROWS : ROWS + EDGE, :] = after[...]
    rest[ROWS + EDGE :, :] = before[...]


def warp_columns(rowed, col_warp):
    for n in range(4):
        low, high = max(0, 256 * n - 128), min(WIDTH, 256 * n + 384)
        yield (
            n,
            jnp.dot(
                rowed[:, low:high],
                col_warp[low:high, 256 * n : 256 * n + 256],
                preferred_element_type=jnp.float32,
            ).astype(jnp.bfloat16),
        )


def warp_weight_kernel(
    tile,
    level,
    visit_weight,
    flux,
    own,
    far,
    after,
    before,
    row_warp,
    col_warp,
    warped,
    share,
    turn,
    rest,
    rowed,
):
    near, turned = near_columns(tile[0], level[0] == 1, row_warp)
    share[...] = jnp.dot(near, flux[...], preferred_element_type=jnp.float32)
    turn[...] = turned
    gather_rest(rest, far, after.at[pl.ds(EDGE, EDGE)], before.at[pl.ds(EDGE, EDGE)])
    both = jnp.dot(near, own[...], preferred_element_type=jnp.float32) + jnp.dot(
        turned, rest[...], preferred_element_type=jnp.float32
    )
    scale = visit_weight[0].astype(jnp.bfloat16).astype(jnp.float32)
    rowed[...] = (scale * both).astype(jnp.bfloat16)
    for n, part in warp_columns(rowed, col_warp):
        warped[:, 256 * n : 256 * n + 256] = part


def warp_flux_kernel(
    dest_slot,
    share,
    turn,
    far,
    after,
    before,
    col_warp,
    warped_weight,
    notes,
    outgoing,
    rest,
    rowed,
):
    gather_rest(rest, far, after, before)
    rowed[...] = (
        share[...] + jnp.dot(turn[...], rest[...], preferred_element_type=jnp.float32)
    ).astype(jnp.bfloat16)
    outgoing[:, 64:, :] = notes[...]
    for n, part in warp_columns(rowed, col_warp):
        for down in range(8):
            for c in range(2):
                column = 2 * n + c
                slot = dest_slot[down * 8 + column]
                owner, at = slot // 2, pl.multiple_of(lax.rem(slot, 2) * 32, 32)
                rows = slice(down * 16, down * 16 + 16)
                outgoing[owner, pl.ds(at, 16), :] = part[rows, c * 128 : c * 128 + 128]
                outgoing[owner, pl.ds(at + 16, 16), :] = warped_weight[
                    rows, column * 128 : column * 128 + 128
                ]


def patch_kernel(arriving, coadd, reply, sums, values, served, note, table, sem, out_sem):
    notes = arriving[0, 64:, :].astype(jnp.float32)
    for sender in range(1, 64):
        notes = notes + arriving[sender, 64:, :].astype(jnp.float32)
    note[...] = notes.astype(jnp.int32)
    copy = pltpu.make_async_copy(note, table, sem)
    copy.start()
    sums[...] = jnp.zeros_like(sums)
    copy.wait()

    def add(sender, _):
        for rank in range(2):
            at = table[0, 2 * sender + rank]
            sums[at] = sums[at] + arriving[sender, rank * 32 : rank * 32 + 32, :].astype(jnp.float32)
        return 0

    lax.fori_loop(0, 64, add, 0, unroll=4)
    for block in range(NBLK):
        down, c = block // 8, block % 8
        value = sums[block, :16, :] / jnp.maximum(sums[block, 16:, :], FLOOR)
        values[down * 16 : down * 16 + 16, c * 128 : c * 128 + 128] = value
        served[block] = value.astype(jnp.bfloat16)
    out = pltpu.make_async_copy(values, coadd, out_sem)
    out.start()

    def serve(sender, _):
        for rank in range(2):
            reply[2 * sender + rank] = served[table[1, 2 * sender + rank]]
        return 0

    lax.fori_loop(0, 64, serve, 0, unroll=4)
    out.wait()


def difference_kernel(tmpl_slot, returned, new_science, difference, held, sems):
    copies = []
    for down in range(8):
        rows = slice(down * 16, down * 16 + 16)
        for c in range(8):
            columns = slice(c * 128, c * 128 + 128)
            template = returned[tmpl_slot[down * 8 + c]].astype(jnp.float32)
            held[rows, columns] = new_science[rows, columns] - template
        if down % 2 == 1:
            part = pl.ds(down * 16 - 16, 32)
            copies.append(
                pltpu.make_async_copy(held.at[part], difference.at[part], sems.at[down // 2])
            )
            copies[-1].start()
    for copy in copies:
        copy.wait()


def per_device(
    visit_image,
    mask_bits,
    visit_weight,
    basis_cols,
    basis_rows,
    kernel_coef,
    row_warp,
    col_warp,
    dest_owner,
    dest_block,
    new_science,
    tmpl_owner,
    tmpl_block,
):
    f32, bf16, i32 = jnp.float32, jnp.bfloat16, jnp.int32
    struct = jax.ShapeDtypeStruct
    tile = lax.axis_index("tile").astype(i32).reshape(1)
    home = lax.axis_index("ccd").astype(i32).reshape(1)
    up = [(i, (i + 1) % NTILE) for i in range(NTILE)]
    down = [(i, (i + 3) % NTILE) for i in range(NTILE)]
    across = [(i, (i + 2) % NTILE) for i in range(NTILE)]

    to_next, to_previous, good, coef, cols_t, rows_t, level = call(
        edge_kernel,
        (
            struct((2 * EDGE, WIDTH), bf16),
            struct((2 * EDGE, WIDTH), bf16),
            struct((ROWS, WIDTH), bf16),
            struct((6, 1, NB), f32),
            struct((TAPS, NB), bf16),
            struct((TAPS, NB), bf16),
            struct((8,), i32),
        ),
        [SMEM] + [HBM] * 6,
        (VMEM,) * 6 + (SMEM,),
        [
            pltpu.VMEM((ROWS, WIDTH), i32),
            pltpu.VMEM((ROWS, ROWS), bf16),
            pltpu.SemaphoreType.DMA((11,)),
        ],
        "edges",
        400_000,
        1_000_000,
    )(
        tile,
        in_hbm(visit_image),
        in_hbm(mask_bits),
        in_hbm(row_warp),
        in_hbm(kernel_coef.transpose(2, 0, 1)),
        in_hbm(basis_cols.T),
        in_hbm(basis_rows.T),
    )
    before = lax.ppermute(to_next, "tile", up)
    after = lax.ppermute(to_previous, "tile", down)
    later_good, before, after = lax.optimization_barrier((good, before, after))
    far_good = lax.ppermute(later_good, "tile", across)

    dest_slot, tmpl_slot, notes = call(
        index_kernel,
        (struct((64,), i32), struct((64,), i32), struct((64, NOTE, 128), bf16)),
        [SMEM] * 5,
        (SMEM, SMEM, VMEM),
        [pltpu.SMEM((128,), i32), pltpu.SMEM((256,), i32)],
        "slots",
        2_000_000,
        1_000_000,
    )(home, dest_owner[:, 0], dest_block, tmpl_owner[:, 0], tmpl_block)

    taps = call(
        table_kernel,
        struct((2, 3 * BAND, DEPTH), bf16),
        [SMEM, VMEM, VMEM, VMEM],
        VMEM,
        [pltpu.VMEM((128, NB), f32)],
        "taps",
        10_000_000,
        2_000_000,
    )(tile, coef, cols_t, rows_t)
    flux, flux_to_next, flux_to_previous = call(
        conv_kernel,
        (struct((ROWS, WIDTH), bf16),) + (struct((EDGE, WIDTH), bf16),) * 2,
        [SMEM] * 3 + [VMEM] * 5,
        (VMEM,) * 3,
        [pltpu.VMEM((2, DEPTH, WIDTH), bf16)],
        "matching",
        2 * 2 * 192 * DEPTH * WIDTH,
        3_000_000,
    )(tile, level, visit_weight, before, visit_image, after, taps, good)
    far_flux = lax.ppermute(flux, "tile", across)
    after_flux = lax.ppermute(flux_to_previous, "tile", down)
    before_flux = lax.ppermute(flux_to_next, "tile", up)
    reach = ROWS + 2 * EDGE
    scratch = [pltpu.VMEM((reach, WIDTH), bf16), pltpu.VMEM((ROWS, WIDTH), bf16)]
    warped_weight, share, turn = call(
        warp_weight_kernel,
        (struct((ROWS, WIDTH), bf16), struct((ROWS, WIDTH), f32), struct((ROWS, reach), bf16)),
        [SMEM] * 3 + [VMEM] * 7,
        (VMEM,) * 3,
        scratch,
        "warp_weight",
        2 * 128 * WIDTH * WIDTH,
        4_000_000,
    )(tile, level, visit_weight, flux, good, far_good, after, before, row_warp, col_warp[0])
    outgoing = call(
        warp_flux_kernel,
        struct((64, MESSAGE, 128), bf16),
        [SMEM] + [VMEM] * 8,
        VMEM,
        scratch,
        "warp_flux",
        2 * 128 * WIDTH * WIDTH,
        5_000_000,
    )(
        dest_slot,
        share,
        turn,
        far_flux,
        after_flux,
        before_flux,
        col_warp[0],
        warped_weight,
        notes,
    )
    arriving = lax.all_to_all(outgoing, "ccd", split_axis=0, concat_axis=0, tiled=True)
    coadd, reply = call(
        patch_kernel,
        (struct((ROWS, WIDTH), f32), struct((SLOTS, 16, 128), bf16)),
        [VMEM],
        (HBM, VMEM),
        [
            pltpu.VMEM((NBLK + 8, 32, 128), f32),
            pltpu.VMEM((ROWS, WIDTH), f32),
            pltpu.VMEM((NBLK, 16, 128), bf16),
            pltpu.VMEM((NOTE, 128), i32),
            pltpu.SMEM((NOTE, 128), i32),
            pltpu.SemaphoreType.DMA,
            pltpu.SemaphoreType.DMA,
        ],
        "patch",
        1_000_000,
        2_000_000,
    )(arriving)
    returned = lax.all_to_all(reply, "ccd", split_axis=0, concat_axis=0, tiled=True)
    difference = call(
        difference_kernel,
        struct((ROWS, WIDTH), f32),
        [SMEM, VMEM, VMEM],
        HBM,
        [pltpu.VMEM((ROWS, WIDTH), f32), pltpu.SemaphoreType.DMA((4,))],
        "difference",
        1_000_000,
        2_000_000,
    )(tmpl_slot, returned, new_science)
    return coadd, difference


def solution(mesh):
    both = P(("ccd", "tile"), None)
    return jax.shard_map(
        per_device,
        mesh=mesh,
        in_specs=(
            both,
            both,
            P("ccd"),
            P(),
            P(),
            P("ccd", None, None),
            both,
            P("ccd", None, None),
            both,
            P(("ccd", "tile")),
            both,
            both,
            P(("ccd", "tile")),
        ),
        out_specs=(both, both),
        check_vma=False,
    )
```

```python
import functools

import jax
import jax.numpy as jnp
from jax import lax
from jax.experimental import pallas as pl
from jax.experimental.pallas import tpu as pltpu
from jax.sharding import PartitionSpec as P

BLOCK_ROWS = 16
BLOCK_COLUMNS = 128
FLOOR = 1.0

ROWS = 128
WIDTH = 1024
CUTOUT = 512
NTILE = 4
NB = 31
TAPS = 21
HALF = 10
EDGE = 16
BAND = 64
WINDOW = 96
DEPTH = 2048
USED = TAPS * WINDOW
NBLK = 64
SLOTS = 128
NOTE = 8
MESSAGE = 64 + NOTE

VMEM = pl.BlockSpec(memory_space=pltpu.VMEM)
HBM = pl.BlockSpec(memory_space=pltpu.HBM)
SMEM = pl.BlockSpec(memory_space=pltpu.SMEM)


def in_hbm(array):
    return pltpu.with_memory_space_constraint(array, pltpu.HBM)


def call(body, out_shape, in_specs, out_specs, scratch, name, flops, nbytes):
    return pl.pallas_call(
        body,
        out_shape=out_shape,
        in_specs=in_specs,
        out_specs=out_specs,
        scratch_shapes=scratch,
        name=name,
        compiler_params=pltpu.CompilerParams(vmem_limit_bytes=20 * 1024 * 1024),
        cost_estimate=pl.CostEstimate(flops=flops, bytes_accessed=nbytes, transcendentals=0),
    )


def index_kernel(
    home,
    dest_owner,
    dest_block,
    tmpl_owner,
    tmpl_block,
    dest_slot,
    tmpl_slot,
    notes,
    count,
    table,
):
    def clear(i, _):
        count[i] = 0
        count[64 + i] = 0
        table[4 * i] = NBLK
        table[4 * i + 1] = NBLK
        table[4 * i + 2] = 0
        table[4 * i + 3] = 0
        return 0

    lax.fori_loop(0, 64, clear, 0, unroll=8)

    def place(k, _):
        owner = dest_owner[k]
        rank = count[owner]
        count[owner] = rank + 1
        dest_slot[k] = 2 * owner + rank
        table[4 * owner + rank] = dest_block[k]
        asked = tmpl_owner[k]
        rank = count[64 + asked]
        count[64 + asked] = rank + 1
        tmpl_slot[k] = 2 * asked + rank
        table[4 * asked + 2 + rank] = tmpl_block[k]
        return 0

    lax.fori_loop(0, 64, place, 0, unroll=8)

    row = lax.broadcasted_iota(jnp.int32, (NOTE, 128), 0)
    lane = lax.broadcasted_iota(jnp.int32, (NOTE, 128), 1) - 2 * home[0]
    for patch in range(64):
        note = jnp.zeros((NOTE, 128), jnp.int32)
        for kind in range(2):
            for rank in range(2):
                here = (row == kind) & (lane == rank)
                note = jnp.where(here, table[4 * patch + 2 * kind + rank], note)
        notes[patch] = note.astype(jnp.float32).astype(jnp.bfloat16)


def table_kernel(tile, coef, cols_t, rows_t, table, wide):
    wide[...] = jnp.zeros_like(wide)
    wide[6 : 6 + TAPS, :] = cols_t[...].astype(jnp.float32)
    taps = []
    for p in range(6):
        taps.append(
            lax.dot_general(
                rows_t[...].astype(jnp.float32) * coef[p],
                wide[...],
                (((1,), (1,)), ((), ())),
                preferred_element_type=jnp.float32,
                precision=lax.Precision.HIGHEST,
            )
        )
    lane = lax.broadcasted_iota(jnp.int32, (BAND, 128), 1)
    row = lax.broadcasted_iota(jnp.int32, (BAND, 128), 0)
    for band in range(2):
        first = tile[0] * ROWS + band * BAND
        yn = (2.0 * (first + row).astype(jnp.float32) + 1.0) / CUTOUT - 1.0
        yy = yn * yn

        def turned(i):
            v = [jnp.broadcast_to(taps[p][i : i + 1, :], (BAND, 128)) for p in range(6)]
            mixed = (v[0] + yn * v[1] + yy * v[3], v[2] + yn * v[4], v[5])
            return [
                pltpu.roll(m, (i * WINDOW) % 128, 1, stride=1, stride_axis=0) for m in mixed
            ]

        held = {}
        for column in range(DEPTH // 128):
            left = (128 * column) // WINDOW
            bound = (left + 1) * WINDOW - 128 * column
            for i in (left, left + 1):
                if i < TAPS and i not in held:
                    held[i] = turned(i)
            for q in range(3):
                other = held[left + 1][q] if left + 1 < TAPS else jnp.zeros((BAND, 128), jnp.float32)
                table[band, q * BAND : (q + 1) * BAND, column * 128 : (column + 1) * 128] = jnp.where(
                    lane < bound, held[left][q], other
                ).astype(jnp.bfloat16)
            held = {i: held[i] for i in held if i > left}


def edge_kernel(
    tile,
    image,
    mask,
    row_warp,
    coef,
    cols,
    rows,
    to_next,
    to_previous,
    good,
    coef_near,
    cols_near,
    rows_near,
    level,
    held,
    own_part,
    sems,
):
    last = ROWS - EDGE
    copies = []
    parts = [(0, EDGE), (last, EDGE)] + [(EDGE + 32 * part, 32) for part in range(3)]
    for first, count in parts[:2]:
        span = pl.ds(first, count)
        copies.append(pltpu.make_async_copy(mask.at[span], held.at[span], sems.at[len(copies)]))
    copies.append(
        pltpu.make_async_copy(image.at[pl.ds(last, EDGE)], to_next.at[pl.ds(0, EDGE)], sems.at[2])
    )
    copies.append(
        pltpu.make_async_copy(image.at[pl.ds(0, EDGE)], to_previous.at[pl.ds(0, EDGE)], sems.at[3])
    )
    for first, count in parts[2:]:
        span = pl.ds(first, count)
        copies.append(pltpu.make_async_copy(mask.at[span], held.at[span], sems.at[len(copies)]))
    own_columns = pl.ds(pl.multiple_of(tile[0] * ROWS, ROWS), ROWS)
    for source, near in (
        (coef, coef_near),
        (cols, cols_near),
        (rows, rows_near),
    ):
        copies.append(pltpu.make_async_copy(source, near, sems.at[len(copies)]))
    middle = pltpu.make_async_copy(
        row_warp.at[pl.ds(ROWS // 2, EDGE), own_columns], own_part, sems.at[len(copies)]
    )
    middle.start()
    for copy in copies:
        copy.start()
    middle.wait()
    size = jnp.abs(own_part[...].astype(jnp.float32))
    level[...] = jnp.broadcast_to(jnp.max(size, axis=(0, 1), keepdims=True), level.shape)
    for (first, count), copy in zip(parts, copies[:2] + copies[4:7]):
        copy.wait()
        span = slice(first, first + count)
        flags = jnp.where(jnp.bitwise_and(held[span, :], 3) == 3, 0.0, 1.0)
        good[span, :] = flags.astype(jnp.bfloat16)
    for copy in copies[2:4] + copies[7:]:
        copy.wait()
    send_ends(level, good, to_next.at[pl.ds(EDGE, EDGE)], to_previous.at[pl.ds(EDGE, EDGE)])


def send_ends(level, plane, to_next, to_previous):
    is_level = jnp.broadcast_to(level[:1, :1] > 0.0, (EDGE, WIDTH))
    head, tail = plane[:EDGE, :].astype(jnp.float32), plane[ROWS - EDGE :, :].astype(jnp.float32)
    to_next[...] = jnp.where(is_level, tail, head).astype(jnp.bfloat16)
    to_previous[...] = jnp.where(is_level, head, tail).astype(jnp.bfloat16)


def conv_kernel(
    tile, visit_weight, level, before, image, after, table, good, flux, to_next, to_previous, stack
):
    t = tile[0]
    for group in range(10):
        if group == 0:
            strip = jnp.where(t > 0, before[:EDGE, :].astype(jnp.float32), 0.0)
        elif group == 9:
            strip = jnp.where(t < NTILE - 1, after[:EDGE, :].astype(jnp.float32), 0.0)
        else:
            strip = image[(group - 1) * 16 : group * 16, :].astype(jnp.float32)
        strip = jnp.concatenate([strip, jnp.zeros((16, 128), jnp.float32)], axis=1)
        for i in range(TAPS):
            moved = strip if i == HALF else pltpu.roll(strip, (HALF - i) % (WIDTH + 128), 1)
            moved = moved[:, :WIDTH].astype(jnp.bfloat16)
            if group < 6:
                at = i * WINDOW + group * 16
                stack[0, at : at + 16, :] = moved
            if group >= 4:
                at = i * WINDOW + group * 16 - BAND
                stack[1, at : at + 16, :] = moved
    stack[:, USED:, :] = jnp.zeros((2, DEPTH - USED, WIDTH), jnp.bfloat16)
    scale = visit_weight[0].astype(jnp.bfloat16).astype(jnp.float32)
    for band in range(2):
        rows = slice(band * BAND, (band + 1) * BAND)
        for n in range(4):
            columns = slice(n * 256, (n + 1) * 256)
            parts = jnp.dot(
                table[band], stack[band, :, columns], preferred_element_type=jnp.float32
            )
            x = lax.broadcasted_iota(jnp.int32, (BAND, 256), 1) + n * 256
            xn = (2.0 * x.astype(jnp.float32) + 1.0) / WIDTH - 1.0
            conv = parts[:BAND] + xn * (parts[BAND : 2 * BAND] + xn * parts[2 * BAND :])
            weight = scale * good[rows, columns].astype(jnp.float32)
            flux[rows, columns] = (weight * conv).astype(jnp.bfloat16)
    send_ends(level, flux, to_next, to_previous)


def near_columns(t, level, row_warp):
    def columns(block):
        return row_warp[:, pl.ds(pl.multiple_of(lax.rem(block, NTILE) * ROWS, ROWS), ROWS)]

    is_level = jnp.broadcast_to(level[:1, :1] > 0.0, (ROWS, EDGE))

    def end(block, first_if_level):
        part = columns(block).astype(jnp.float32)
        first, last = part[:, :EDGE], part[:, ROWS - EDGE :]
        chosen = (first, last) if first_if_level else (last, first)
        return jnp.where(is_level, chosen[0], chosen[1]).astype(jnp.bfloat16)

    parts = [columns(t + 2), end(t + 1, True), end(t + 3, False)]
    return columns(t), jnp.concatenate(parts, axis=1)


def gather_rest(rest, far, after, before):
    rest[:ROWS, :] = far[...]
    rest[ROWS : ROWS + EDGE, :] = after[...]
    rest[ROWS + EDGE :, :] = before[...]


def warp_columns(rowed, col_warp):
    for n in range(4):
        low, high = max(0, 256 * n - 128), min(WIDTH, 256 * n + 384)
        yield (
            n,
            jnp.dot(
                rowed[:, low:high],
                col_warp[low:high, 256 * n : 256 * n + 256],
                preferred_element_type=jnp.float32,
            ).astype(jnp.bfloat16),
        )


def warp_weight_kernel(
    tile,
    visit_weight,
    level,
    flux,
    own,
    far,
    after,
    before,
    row_warp,
    col_warp,
    warped,
    share,
    turn,
    rest,
    rowed,
):
    near, turned = near_columns(tile[0], level, row_warp)
    share[...] = jnp.dot(near, flux[...], preferred_element_type=jnp.float32)
    turn[...] = turned
    gather_rest(rest, far, after.at[pl.ds(EDGE, EDGE)], before.at[pl.ds(EDGE, EDGE)])
    both = jnp.dot(near, own[...], preferred_element_type=jnp.float32) + jnp.dot(
        turned, rest[...], preferred_element_type=jnp.float32
    )
    scale = visit_weight[0].astype(jnp.bfloat16).astype(jnp.float32)
    rowed[...] = (scale * both).astype(jnp.bfloat16)
    for n, part in warp_columns(rowed, col_warp):
        warped[:, 256 * n : 256 * n + 256] = part


def warp_flux_kernel(
    dest_slot_in,
    share,
    turn,
    far,
    after,
    before,
    col_warp,
    warped_weight,
    notes,
    outgoing,
    rest,
    rowed,
    dest_slot,
    sem,
):
    copy = pltpu.make_async_copy(dest_slot_in, dest_slot, sem)
    copy.start()
    gather_rest(rest, far, after, before)
    rowed[...] = (
        share[...] + jnp.dot(turn[...], rest[...], preferred_element_type=jnp.float32)
    ).astype(jnp.bfloat16)
    outgoing[:, 64:, :] = notes[...]
    copy.wait()
    for n, part in warp_columns(rowed, col_warp):
        for down in range(8):
            for c in range(2):
                column = 2 * n + c
                slot = dest_slot[down * 8 + column]
                owner, at = slot // 2, pl.multiple_of(lax.rem(slot, 2) * 32, 32)
                rows = slice(down * 16, down * 16 + 16)
                outgoing[owner, pl.ds(at, 16), :] = part[rows, c * 128 : c * 128 + 128]
                outgoing[owner, pl.ds(at + 16, 16), :] = warped_weight[
                    rows, column * 128 : column * 128 + 128
                ]


def patch_kernel(arriving, coadd, reply, sums, values, served, note, table, sem, out_sem):
    notes = arriving[0, 64:, :].astype(jnp.float32)
    for sender in range(1, 64):
        notes = notes + arriving[sender, 64:, :].astype(jnp.float32)
    note[...] = notes.astype(jnp.int32)
    copy = pltpu.make_async_copy(note, table, sem)
    copy.start()
    sums[...] = jnp.zeros_like(sums)
    copy.wait()

    def add(sender, _):
        for rank in range(2):
            at = table[0, 2 * sender + rank]
            sums[at] = sums[at] + arriving[sender, rank * 32 : rank * 32 + 32, :].astype(jnp.float32)
        return 0

    lax.fori_loop(0, 64, add, 0, unroll=4)
    for block in range(NBLK):
        down, c = block // 8, block % 8
        value = sums[block, :16, :] / jnp.maximum(sums[block, 16:, :], FLOOR)
        values[down * 16 : down * 16 + 16, c * 128 : c * 128 + 128] = value
        served[block] = value.astype(jnp.bfloat16)
    out = pltpu.make_async_copy(values, coadd, out_sem)
    out.start()

    def serve(sender, _):
        for rank in range(2):
            reply[2 * sender + rank] = served[table[1, 2 * sender + rank]]
        return 0

    lax.fori_loop(0, 64, serve, 0, unroll=4)
    out.wait()


def difference_kernel(tmpl_slot, returned, new_science, difference, held, sems):
    copies = []
    for down in range(8):
        rows = slice(down * 16, down * 16 + 16)
        for c in range(8):
            columns = slice(c * 128, c * 128 + 128)
            template = returned[tmpl_slot[down * 8 + c]].astype(jnp.float32)
            held[rows, columns] = new_science[rows, columns] - template
        if down % 2 == 1:
            part = pl.ds(down * 16 - 16, 32)
            copies.append(
                pltpu.make_async_copy(held.at[part], difference.at[part], sems.at[down // 2])
            )
            copies[-1].start()
    for copy in copies:
        copy.wait()


def per_device(
    visit_image,
    mask_bits,
    visit_weight,
    basis_cols,
    basis_rows,
    kernel_coef,
    row_warp,
    col_warp,
    dest_owner,
    dest_block,
    new_science,
    tmpl_owner,
    tmpl_block,
):
    f32, bf16, i32 = jnp.float32, jnp.bfloat16, jnp.int32
    struct = jax.ShapeDtypeStruct
    tile = lax.axis_index("tile").astype(i32).reshape(1)
    home = lax.axis_index("ccd").astype(i32).reshape(1)
    up = [(i, (i + 1) % NTILE) for i in range(NTILE)]
    down = [(i, (i + 3) % NTILE) for i in range(NTILE)]
    across = [(i, (i + 2) % NTILE) for i in range(NTILE)]

    to_next, to_previous, good, coef, cols_t, rows_t, level = call(
        edge_kernel,
        (
            struct((2 * EDGE, WIDTH), bf16),
            struct((2 * EDGE, WIDTH), bf16),
            struct((ROWS, WIDTH), bf16),
            struct((6, 1, NB), f32),
            struct((TAPS, NB), bf16),
            struct((TAPS, NB), bf16),
            struct((8, 128), f32),
        ),
        [SMEM] + [HBM] * 6,
        (VMEM,) * 7,
        [
            pltpu.VMEM((ROWS, WIDTH), i32),
            pltpu.VMEM((EDGE, ROWS), bf16),
            pltpu.SemaphoreType.DMA((11,)),
        ],
        "edges",
        400_000,
        1_000_000,
    )(
        tile,
        in_hbm(visit_image),
        in_hbm(mask_bits),
        in_hbm(row_warp),
        in_hbm(kernel_coef.transpose(2, 0, 1)),
        in_hbm(basis_cols.T),
        in_hbm(basis_rows.T),
    )
    before = lax.ppermute(to_next, "tile", up)
    after = lax.ppermute(to_previous, "tile", down)

    dest_slot, tmpl_slot, notes = call(
        index_kernel,
        (struct((64,), i32), struct((64,), i32), struct((64, NOTE, 128), bf16)),
        [SMEM] * 5,
        (SMEM, SMEM, VMEM),
        [pltpu.SMEM((128,), i32), pltpu.SMEM((256,), i32)],
        "slots",
        2_000_000,
        1_000_000,
    )(home, dest_owner[:, 0], dest_block, tmpl_owner[:, 0], tmpl_block)

    taps = call(
        table_kernel,
        struct((2, 3 * BAND, DEPTH), bf16),
        [SMEM, VMEM, VMEM, VMEM],
        VMEM,
        [pltpu.VMEM((128, NB), f32)],
        "taps",
        10_000_000,
        2_000_000,
    )(tile, coef, cols_t, rows_t)
    later_good, taps = lax.optimization_barrier((good, taps))
    far_good = lax.ppermute(later_good, "tile", across)
    flux, flux_to_next, flux_to_previous = call(
        conv_kernel,
        (struct((ROWS, WIDTH), bf16),) + (struct((EDGE, WIDTH), bf16),) * 2,
        [SMEM] * 2 + [VMEM] * 6,
        (VMEM,) * 3,
        [pltpu.VMEM((2, DEPTH, WIDTH), bf16)],
        "matching",
        2 * 2 * 192 * DEPTH * WIDTH,
        3_000_000,
    )(tile, visit_weight, level, before, visit_image, after, taps, good)
    far_flux = lax.ppermute(flux, "tile", across)
    after_flux = lax.ppermute(flux_to_previous, "tile", down)
    before_flux = lax.ppermute(flux_to_next, "tile", up)
    reach = ROWS + 2 * EDGE
    scratch = [pltpu.VMEM((reach, WIDTH), bf16), pltpu.VMEM((ROWS, WIDTH), bf16)]
    warped_weight, share, turn = call(
        warp_weight_kernel,
        (struct((ROWS, WIDTH), bf16), struct((ROWS, WIDTH), f32), struct((ROWS, reach), bf16)),
        [SMEM] * 2 + [VMEM] * 8,
        (VMEM,) * 3,
        scratch,
        "warp_weight",
        2 * 128 * WIDTH * WIDTH,
        4_000_000,
    )(tile, visit_weight, level, flux, good, far_good, after, before, row_warp, col_warp[0])
    outgoing = call(
        warp_flux_kernel,
        struct((64, MESSAGE, 128), bf16),
        [VMEM] * 9,
        VMEM,
        scratch + [pltpu.SMEM((64,), i32), pltpu.SemaphoreType.DMA],
        "warp_flux",
        2 * 128 * WIDTH * WIDTH,
        5_000_000,
    )(
        dest_slot,
        share,
        turn,
        far_flux,
        after_flux,
        before_flux,
        col_warp[0],
        warped_weight,
        notes,
    )
    arriving = lax.all_to_all(outgoing, "ccd", split_axis=0, concat_axis=0, tiled=True)
    coadd, reply = call(
        patch_kernel,
        (struct((ROWS, WIDTH), f32), struct((SLOTS, 16, 128), bf16)),
        [VMEM],
        (HBM, VMEM),
        [
            pltpu.VMEM((NBLK + 8, 32, 128), f32),
            pltpu.VMEM((ROWS, WIDTH), f32),
            pltpu.VMEM((NBLK, 16, 128), bf16),
            pltpu.VMEM((NOTE, 128), i32),
            pltpu.SMEM((NOTE, 128), i32),
            pltpu.SemaphoreType.DMA,
            pltpu.SemaphoreType.DMA,
        ],
        "patch",
        1_000_000,
        2_000_000,
    )(arriving)
    returned = lax.all_to_all(reply, "ccd", split_axis=0, concat_axis=0, tiled=True)
    difference = call(
        difference_kernel,
        struct((ROWS, WIDTH), f32),
        [SMEM, VMEM, VMEM],
        HBM,
        [pltpu.VMEM((ROWS, WIDTH), f32), pltpu.SemaphoreType.DMA((4,))],
        "difference",
        1_000_000,
        2_000_000,
    )(tmpl_slot, returned, new_science)
    return coadd, difference


def solution(mesh):
    both = P(("ccd", "tile"), None)
    return jax.shard_map(
        per_device,
        mesh=mesh,
        in_specs=(
            both,
            both,
            P("ccd"),
            P(),
            P(),
            P("ccd", None, None),
            both,
            P("ccd", None, None),
            both,
            P(("ccd", "tile")),
            both,
            both,
            P(("ccd", "tile")),
        ),
        out_specs=(both, both),
        check_vma=False,
    )
```

```python
import functools

import jax
import jax.numpy as jnp
from jax import lax
from jax.experimental import pallas as pl
from jax.experimental.pallas import tpu as pltpu
from jax.sharding import PartitionSpec as P

BLOCK_ROWS = 16
BLOCK_COLUMNS = 128
FLOOR = 1.0

ROWS = 128
WIDTH = 1024
CUTOUT = 512
NTILE = 4
NB = 31
TAPS = 21
HALF = 10
EDGE = 16
BAND = 64
WINDOW = 96
DEPTH = 2048
USED = TAPS * WINDOW
NBLK = 64
SLOTS = 128
NOTE = 8
MESSAGE = 64 + NOTE

VMEM = pl.BlockSpec(memory_space=pltpu.VMEM)
HBM = pl.BlockSpec(memory_space=pltpu.HBM)
SMEM = pl.BlockSpec(memory_space=pltpu.SMEM)


def in_hbm(array):
    return pltpu.with_memory_space_constraint(array, pltpu.HBM)


def call(body, out_shape, in_specs, out_specs, scratch, name, flops, nbytes):
    return pl.pallas_call(
        body,
        out_shape=out_shape,
        in_specs=in_specs,
        out_specs=out_specs,
        scratch_shapes=scratch,
        name=name,
        compiler_params=pltpu.CompilerParams(vmem_limit_bytes=20 * 1024 * 1024),
        cost_estimate=pl.CostEstimate(flops=flops, bytes_accessed=nbytes, transcendentals=0),
    )


def index_kernel(
    home,
    dest_owner,
    dest_block,
    tmpl_owner,
    tmpl_block,
    dest_slot,
    tmpl_slot,
    notes,
    count,
    table,
):
    def clear(i, _):
        count[i] = 0
        count[64 + i] = 0
        table[4 * i] = NBLK
        table[4 * i + 1] = NBLK
        table[4 * i + 2] = 0
        table[4 * i + 3] = 0
        return 0

    lax.fori_loop(0, 64, clear, 0, unroll=8)

    def place(k, _):
        owner = dest_owner[k]
        rank = count[owner]
        count[owner] = rank + 1
        dest_slot[k] = 2 * owner + rank
        table[4 * owner + rank] = dest_block[k]
        asked = tmpl_owner[k]
        rank = count[64 + asked]
        count[64 + asked] = rank + 1
        tmpl_slot[k] = 2 * asked + rank
        table[4 * asked + 2 + rank] = tmpl_block[k]
        return 0

    lax.fori_loop(0, 64, place, 0, unroll=8)

    row = lax.broadcasted_iota(jnp.int32, (NOTE, 128), 0)
    lane = lax.broadcasted_iota(jnp.int32, (NOTE, 128), 1) - 2 * home[0]
    for patch in range(64):
        note = jnp.zeros((NOTE, 128), jnp.int32)
        for kind in range(2):
            for rank in range(2):
                here = (row == kind) & (lane == rank)
                note = jnp.where(here, table[4 * patch + 2 * kind + rank], note)
        notes[patch] = note.astype(jnp.float32).astype(jnp.bfloat16)


def table_kernel(tile, coef, cols_t, rows_t, table, wide, mixed_rows):
    wide[...] = jnp.zeros_like(wide)
    mixed_rows[...] = jnp.zeros_like(mixed_rows)
    wide[6 : 6 + TAPS, :] = cols_t[...].astype(jnp.float32)
    for p in range(6):
        mixed_rows[24 * p : 24 * p + TAPS, :] = rows_t[...].astype(jnp.float32) * coef[p]
    every = lax.dot_general(
        mixed_rows[...],
        wide[...],
        (((1,), (1,)), ((), ())),
        preferred_element_type=jnp.float32,
        precision=lax.Precision.HIGHEST,
    )
    taps = [every[24 * p : 24 * p + TAPS] for p in range(6)]
    lane = lax.broadcasted_iota(jnp.int32, (BAND, 128), 1)
    row = lax.broadcasted_iota(jnp.int32, (BAND, 128), 0)
    for band in range(2):
        first = tile[0] * ROWS + band * BAND
        yn = (2.0 * (first + row).astype(jnp.float32) + 1.0) / CUTOUT - 1.0
        yy = yn * yn

        def turned(i):
            v = [jnp.broadcast_to(taps[p][i : i + 1, :], (BAND, 128)) for p in range(6)]
            mixed = (v[0] + yn * v[1] + yy * v[3], v[2] + yn * v[4], v[5])
            return [
                pltpu.roll(m, (i * WINDOW) % 128, 1, stride=1, stride_axis=0) for m in mixed
            ]

        held = {}
        for column in range(DEPTH // 128):
            left = (128 * column) // WINDOW
            bound = (left + 1) * WINDOW - 128 * column
            for i in (left, left + 1):
                if i < TAPS and i not in held:
                    held[i] = turned(i)
            for q in range(3):
                other = held[left + 1][q] if left + 1 < TAPS else jnp.zeros((BAND, 128), jnp.float32)
                table[band, q * BAND : (q + 1) * BAND, column * 128 : (column + 1) * 128] = jnp.where(
                    lane < bound, held[left][q], other
                ).astype(jnp.bfloat16)
            held = {i: held[i] for i in held if i > left}


def edge_kernel(
    tile,
    image,
    mask,
    row_warp,
    coef,
    cols,
    rows,
    to_next,
    to_previous,
    good,
    coef_near,
    cols_near,
    rows_near,
    level,
    held,
    own_part,
    sems,
):
    last = ROWS - EDGE
    copies = []
    parts = [(0, EDGE), (last, EDGE)] + [(EDGE + 32 * part, 32) for part in range(3)]
    for first, count in parts[:2]:
        span = pl.ds(first, count)
        copies.append(pltpu.make_async_copy(mask.at[span], held.at[span], sems.at[len(copies)]))
    copies.append(
        pltpu.make_async_copy(image.at[pl.ds(last, EDGE)], to_next.at[pl.ds(0, EDGE)], sems.at[2])
    )
    copies.append(
        pltpu.make_async_copy(image.at[pl.ds(0, EDGE)], to_previous.at[pl.ds(0, EDGE)], sems.at[3])
    )
    for first, count in parts[2:]:
        span = pl.ds(first, count)
        copies.append(pltpu.make_async_copy(mask.at[span], held.at[span], sems.at[len(copies)]))
    own_columns = pl.ds(pl.multiple_of(tile[0] * ROWS, ROWS), ROWS)
    for source, near in (
        (coef, coef_near),
        (cols, cols_near),
        (rows, rows_near),
    ):
        copies.append(pltpu.make_async_copy(source, near, sems.at[len(copies)]))
    middle = pltpu.make_async_copy(
        row_warp.at[pl.ds(ROWS // 2, EDGE), own_columns], own_part, sems.at[len(copies)]
    )
    middle.start()
    for copy in copies:
        copy.start()
    middle.wait()
    size = jnp.abs(own_part[...].astype(jnp.float32))
    level[...] = jnp.broadcast_to(jnp.max(size, axis=(0, 1), keepdims=True), level.shape)
    for (first, count), copy in zip(parts, copies[:2] + copies[4:7]):
        copy.wait()
        span = slice(first, first + count)
        flags = jnp.where(jnp.bitwise_and(held[span, :], 3) == 3, 0.0, 1.0)
        good[span, :] = flags.astype(jnp.bfloat16)
    for copy in copies[2:4] + copies[7:]:
        copy.wait()
    send_ends(level, good, to_next.at[pl.ds(EDGE, EDGE)], to_previous.at[pl.ds(EDGE, EDGE)])


def send_ends(level, plane, to_next, to_previous):
    is_level = jnp.broadcast_to(level[:1, :1] > 0.0, (EDGE, WIDTH))
    head, tail = plane[:EDGE, :].astype(jnp.float32), plane[ROWS - EDGE :, :].astype(jnp.float32)
    to_next[...] = jnp.where(is_level, tail, head).astype(jnp.bfloat16)
    to_previous[...] = jnp.where(is_level, head, tail).astype(jnp.bfloat16)


def conv_kernel(
    tile, visit_weight, level, before, image, after, table, good, flux, to_next, to_previous, stack
):
    t = tile[0]
    for group in range(10):
        if group == 0:
            strip = jnp.where(t > 0, before[:EDGE, :].astype(jnp.float32), 0.0)
        elif group == 9:
            strip = jnp.where(t < NTILE - 1, after[:EDGE, :].astype(jnp.float32), 0.0)
        else:
            strip = image[(group - 1) * 16 : group * 16, :].astype(jnp.float32)
        strip = jnp.concatenate([strip, jnp.zeros((16, 128), jnp.float32)], axis=1)
        for i in range(TAPS):
            moved = strip if i == HALF else pltpu.roll(strip, (HALF - i) % (WIDTH + 128), 1)
            moved = moved[:, :WIDTH].astype(jnp.bfloat16)
            if group < 6:
                at = i * WINDOW + group * 16
                stack[0, at : at + 16, :] = moved
            if group >= 4:
                at = i * WINDOW + group * 16 - BAND
                stack[1, at : at + 16, :] = moved
    stack[:, USED:, :] = jnp.zeros((2, DEPTH - USED, WIDTH), jnp.bfloat16)
    scale = visit_weight[0].astype(jnp.bfloat16).astype(jnp.float32)
    for band in range(2):
        rows = slice(band * BAND, (band + 1) * BAND)
        for n in range(4):
            columns = slice(n * 256, (n + 1) * 256)
            parts = jnp.dot(
                table[band], stack[band, :, columns], preferred_element_type=jnp.float32
            )
            x = lax.broadcasted_iota(jnp.int32, (BAND, 256), 1) + n * 256
            xn = (2.0 * x.astype(jnp.float32) + 1.0) / WIDTH - 1.0
            conv = parts[:BAND] + xn * (parts[BAND : 2 * BAND] + xn * parts[2 * BAND :])
            weight = scale * good[rows, columns].astype(jnp.float32)
            flux[rows, columns] = (weight * conv).astype(jnp.bfloat16)
    send_ends(level, flux, to_next, to_previous)


def near_columns(t, level, row_warp):
    def columns(block):
        return row_warp[:, pl.ds(pl.multiple_of(lax.rem(block, NTILE) * ROWS, ROWS), ROWS)]

    is_level = jnp.broadcast_to(level[:1, :1] > 0.0, (ROWS, EDGE))

    def end(block, first_if_level):
        part = columns(block).astype(jnp.float32)
        first, last = part[:, :EDGE], part[:, ROWS - EDGE :]
        chosen = (first, last) if first_if_level else (last, first)
        return jnp.where(is_level, chosen[0], chosen[1]).astype(jnp.bfloat16)

    parts = [columns(t + 2), end(t + 1, True), end(t + 3, False)]
    return columns(t), jnp.concatenate(parts, axis=1)


def gather_rest(rest, far, after, before):
    rest[:ROWS, :] = far[...]
    rest[ROWS : ROWS + EDGE, :] = after[...]
    rest[ROWS + EDGE :, :] = before[...]


def warp_columns(rowed, col_warp):
    for n in range(4):
        low, high = max(0, 256 * n - 128), min(WIDTH, 256 * n + 384)
        yield (
            n,
            jnp.dot(
                rowed[:, low:high],
                col_warp[low:high, 256 * n : 256 * n + 256],
                preferred_element_type=jnp.float32,
            ).astype(jnp.bfloat16),
        )


def warp_weight_kernel(
    tile,
    visit_weight,
    level,
    flux,
    own,
    far,
    after,
    before,
    row_warp,
    col_warp,
    warped,
    share,
    turn,
    rest,
    rowed,
):
    near, turned = near_columns(tile[0], level, row_warp)
    share[...] = jnp.dot(near, flux[...], preferred_element_type=jnp.float32)
    turn[...] = turned
    gather_rest(rest, far, after.at[pl.ds(EDGE, EDGE)], before.at[pl.ds(EDGE, EDGE)])
    both = jnp.dot(near, own[...], preferred_element_type=jnp.float32) + jnp.dot(
        turned, rest[...], preferred_element_type=jnp.float32
    )
    scale = visit_weight[0].astype(jnp.bfloat16).astype(jnp.float32)
    rowed[...] = (scale * both).astype(jnp.bfloat16)
    for n, part in warp_columns(rowed, col_warp):
        warped[:, 256 * n : 256 * n + 256] = part


def warp_flux_kernel(
    dest_slot_in,
    share,
    turn,
    far,
    after,
    before,
    col_warp,
    warped_weight,
    notes,
    outgoing,
    rest,
    rowed,
    dest_slot,
    sem,
):
    copy = pltpu.make_async_copy(dest_slot_in, dest_slot, sem)
    copy.start()
    gather_rest(rest, far, after, before)
    rowed[...] = (
        share[...] + jnp.dot(turn[...], rest[...], preferred_element_type=jnp.float32)
    ).astype(jnp.bfloat16)
    outgoing[:, 64:, :] = notes[...]
    copy.wait()
    for n, part in warp_columns(rowed, col_warp):
        for down in range(8):
            for c in range(2):
                column = 2 * n + c
                slot = dest_slot[down * 8 + column]
                owner, at = slot // 2, pl.multiple_of(lax.rem(slot, 2) * 32, 32)
                rows = slice(down * 16, down * 16 + 16)
                outgoing[owner, pl.ds(at, 16), :] = part[rows, c * 128 : c * 128 + 128]
                outgoing[owner, pl.ds(at + 16, 16), :] = warped_weight[
                    rows, column * 128 : column * 128 + 128
                ]


def patch_kernel(arriving, values, reply, sums, served, note, table, sem):
    notes = arriving[0, 64:, :].astype(jnp.float32)
    for sender in range(1, 64):
        notes = notes + arriving[sender, 64:, :].astype(jnp.float32)
    note[...] = notes.astype(jnp.int32)
    copy = pltpu.make_async_copy(note, table, sem)
    copy.start()
    sums[...] = jnp.zeros_like(sums)
    copy.wait()

    def add(sender, _):
        for rank in range(2):
            at = table[0, 2 * sender + rank]
            sums[at] = sums[at] + arriving[sender, rank * 32 : rank * 32 + 32, :].astype(jnp.float32)
        return 0

    lax.fori_loop(0, 64, add, 0, unroll=4)
    for block in range(NBLK):
        down, c = block // 8, block % 8
        value = sums[block, :16, :] / jnp.maximum(sums[block, 16:, :], FLOOR)
        values[down * 16 : down * 16 + 16, c * 128 : c * 128 + 128] = value
        served[block] = value.astype(jnp.bfloat16)

    def serve(sender, _):
        for rank in range(2):
            reply[2 * sender + rank] = served[table[1, 2 * sender + rank]]
        return 0

    lax.fori_loop(0, 64, serve, 0, unroll=4)


def difference_kernel(tmpl_slot, returned, new_science, values, coadd, difference, held, sems):
    copies = [pltpu.make_async_copy(values, coadd, sems.at[4])]
    copies[0].start()
    for down in range(8):
        rows = slice(down * 16, down * 16 + 16)
        for c in range(8):
            columns = slice(c * 128, c * 128 + 128)
            template = returned[tmpl_slot[down * 8 + c]].astype(jnp.float32)
            held[rows, columns] = new_science[rows, columns] - template
        if down % 2 == 1:
            part = pl.ds(down * 16 - 16, 32)
            copies.append(
                pltpu.make_async_copy(held.at[part], difference.at[part], sems.at[down // 2])
            )
            copies[-1].start()
    for copy in copies:
        copy.wait()


def per_device(
    visit_image,
    mask_bits,
    visit_weight,
    basis_cols,
    basis_rows,
    kernel_coef,
    row_warp,
    col_warp,
    dest_owner,
    dest_block,
    new_science,
    tmpl_owner,
    tmpl_block,
):
    f32, bf16, i32 = jnp.float32, jnp.bfloat16, jnp.int32
    struct = jax.ShapeDtypeStruct
    tile = lax.axis_index("tile").astype(i32).reshape(1)
    home = lax.axis_index("ccd").astype(i32).reshape(1)
    up = [(i, (i + 1) % NTILE) for i in range(NTILE)]
    down = [(i, (i + 3) % NTILE) for i in range(NTILE)]
    across = [(i, (i + 2) % NTILE) for i in range(NTILE)]

    to_next, to_previous, good, coef, cols_t, rows_t, level = call(
        edge_kernel,
        (
            struct((2 * EDGE, WIDTH), bf16),
            struct((2 * EDGE, WIDTH), bf16),
            struct((ROWS, WIDTH), bf16),
            struct((6, 1, NB), f32),
            struct((TAPS, NB), bf16),
            struct((TAPS, NB), bf16),
            struct((8, 128), f32),
        ),
        [SMEM] + [HBM] * 6,
        (VMEM,) * 7,
        [
            pltpu.VMEM((ROWS, WIDTH), i32),
            pltpu.VMEM((EDGE, ROWS), bf16),
            pltpu.SemaphoreType.DMA((11,)),
        ],
        "edges",
        400_000,
        1_000_000,
    )(
        tile,
        in_hbm(visit_image),
        in_hbm(mask_bits),
        in_hbm(row_warp),
        in_hbm(kernel_coef.transpose(2, 0, 1)),
        in_hbm(basis_cols.T),
        in_hbm(basis_rows.T),
    )
    before = lax.ppermute(to_next, "tile", up)
    after = lax.ppermute(to_previous, "tile", down)

    dest_slot, tmpl_slot, notes = call(
        index_kernel,
        (struct((64,), i32), struct((64,), i32), struct((64, NOTE, 128), bf16)),
        [SMEM] * 5,
        (SMEM, SMEM, VMEM),
        [pltpu.SMEM((128,), i32), pltpu.SMEM((256,), i32)],
        "slots",
        2_000_000,
        1_000_000,
    )(home, dest_owner[:, 0], dest_block, tmpl_owner[:, 0], tmpl_block)

    taps = call(
        table_kernel,
        struct((2, 3 * BAND, DEPTH), bf16),
        [SMEM, VMEM, VMEM, VMEM],
        VMEM,
        [pltpu.VMEM((128, NB), f32), pltpu.VMEM((144, NB), f32)],
        "taps",
        10_000_000,
        2_000_000,
    )(tile, coef, cols_t, rows_t)
    later_good, taps = lax.optimization_barrier((good, taps))
    far_good = lax.ppermute(later_good, "tile", across)
    flux, flux_to_next, flux_to_previous = call(
        conv_kernel,
        (struct((ROWS, WIDTH), bf16),) + (struct((EDGE, WIDTH), bf16),) * 2,
        [SMEM] * 2 + [VMEM] * 6,
        (VMEM,) * 3,
        [pltpu.VMEM((2, DEPTH, WIDTH), bf16)],
        "matching",
        2 * 2 * 192 * DEPTH * WIDTH,
        3_000_000,
    )(tile, visit_weight, level, before, visit_image, after, taps, good)
    far_flux = lax.ppermute(flux, "tile", across)
    after_flux = lax.ppermute(flux_to_previous, "tile", down)
    before_flux = lax.ppermute(flux_to_next, "tile", up)
    reach = ROWS + 2 * EDGE
    scratch = [pltpu.VMEM((reach, WIDTH), bf16), pltpu.VMEM((ROWS, WIDTH), bf16)]
    warped_weight, share, turn = call(
        warp_weight_kernel,
        (struct((ROWS, WIDTH), bf16), struct((ROWS, WIDTH), f32), struct((ROWS, reach), bf16)),
        [SMEM] * 2 + [VMEM] * 8,
        (VMEM,) * 3,
        scratch,
        "warp_weight",
        2 * 128 * WIDTH * WIDTH,
        4_000_000,
    )(tile, visit_weight, level, flux, good, far_good, after, before, row_warp, col_warp[0])
    outgoing = call(
        warp_flux_kernel,
        struct((64, MESSAGE, 128), bf16),
        [VMEM] * 9,
        VMEM,
        scratch + [pltpu.SMEM((64,), i32), pltpu.SemaphoreType.DMA],
        "warp_flux",
        2 * 128 * WIDTH * WIDTH,
        5_000_000,
    )(
        dest_slot,
        share,
        turn,
        far_flux,
        after_flux,
        before_flux,
        col_warp[0],
        warped_weight,
        notes,
    )
    arriving = lax.all_to_all(outgoing, "ccd", split_axis=0, concat_axis=0, tiled=True)
    values, reply = call(
        patch_kernel,
        (struct((ROWS, WIDTH), f32), struct((SLOTS, 16, 128), bf16)),
        [VMEM],
        (VMEM, VMEM),
        [
            pltpu.VMEM((NBLK + 8, 32, 128), f32),
            pltpu.VMEM((NBLK, 16, 128), bf16),
            pltpu.VMEM((NOTE, 128), i32),
            pltpu.SMEM((NOTE, 128), i32),
            pltpu.SemaphoreType.DMA,
        ],
        "patch",
        1_000_000,
        2_000_000,
    )(arriving)
    returned = lax.all_to_all(reply, "ccd", split_axis=0, concat_axis=0, tiled=True)
    return call(
        difference_kernel,
        (struct((ROWS, WIDTH), f32),) * 2,
        [SMEM, VMEM, VMEM, VMEM],
        (HBM, HBM),
        [pltpu.VMEM((ROWS, WIDTH), f32), pltpu.SemaphoreType.DMA((5,))],
        "difference",
        1_000_000,
        3_000_000,
    )(tmpl_slot, returned, new_science, values)


def solution(mesh):
    both = P(("ccd", "tile"), None)
    return jax.shard_map(
        per_device,
        mesh=mesh,
        in_specs=(
            both,
            both,
            P("ccd"),
            P(),
            P(),
            P("ccd", None, None),
            both,
            P("ccd", None, None),
            both,
            P(("ccd", "tile")),
            both,
            both,
            P(("ccd", "tile")),
        ),
        out_specs=(both, both),
        check_vma=False,
    )
```

```python
import functools

import jax
import jax.numpy as jnp
from jax import lax
from jax.experimental import pallas as pl
from jax.experimental.pallas import tpu as pltpu
from jax.sharding import PartitionSpec as P

BLOCK_ROWS = 16
BLOCK_COLUMNS = 128
FLOOR = 1.0

ROWS = 128
WIDTH = 1024
CUTOUT = 512
NTILE = 4
NB = 31
TAPS = 21
HALF = 10
EDGE = 16
BAND = 64
WINDOW = 96
DEPTH = 2048
USED = TAPS * WINDOW
NBLK = 64
SLOTS = 128
NOTE = 8
MESSAGE = 64 + NOTE

VMEM = pl.BlockSpec(memory_space=pltpu.VMEM)
HBM = pl.BlockSpec(memory_space=pltpu.HBM)
SMEM = pl.BlockSpec(memory_space=pltpu.SMEM)


def in_hbm(array):
    return pltpu.with_memory_space_constraint(array, pltpu.HBM)


def call(body, out_shape, in_specs, out_specs, scratch, name, flops, nbytes):
    return pl.pallas_call(
        body,
        out_shape=out_shape,
        in_specs=in_specs,
        out_specs=out_specs,
        scratch_shapes=scratch,
        name=name,
        compiler_params=pltpu.CompilerParams(vmem_limit_bytes=20 * 1024 * 1024),
        cost_estimate=pl.CostEstimate(flops=flops, bytes_accessed=nbytes, transcendentals=0),
    )


def index_kernel(
    home,
    dest_owner,
    dest_block,
    tmpl_owner,
    tmpl_block,
    dest_slot,
    tmpl_slot,
    notes,
    count,
    table,
):
    def clear(i, _):
        count[i] = 0
        count[64 + i] = 0
        table[4 * i] = NBLK
        table[4 * i + 1] = NBLK
        table[4 * i + 2] = 0
        table[4 * i + 3] = 0
        return 0

    lax.fori_loop(0, 64, clear, 0, unroll=8)

    def place(k, _):
        owner = dest_owner[k]
        rank = count[owner]
        count[owner] = rank + 1
        dest_slot[k] = 2 * owner + rank
        table[4 * owner + rank] = dest_block[k]
        asked = tmpl_owner[k]
        rank = count[64 + asked]
        count[64 + asked] = rank + 1
        tmpl_slot[k] = 2 * asked + rank
        table[4 * asked + 2 + rank] = tmpl_block[k]
        return 0

    lax.fori_loop(0, 64, place, 0, unroll=8)

    row = lax.broadcasted_iota(jnp.int32, (NOTE, 128), 0)
    lane = lax.broadcasted_iota(jnp.int32, (NOTE, 128), 1) - 2 * home[0]
    for patch in range(64):
        note = jnp.zeros((NOTE, 128), jnp.int32)
        for kind in range(2):
            for rank in range(2):
                here = (row == kind) & (lane == rank)
                note = jnp.where(here, table[4 * patch + 2 * kind + rank], note)
        notes[patch] = note.astype(jnp.float32).astype(jnp.bfloat16)


def table_kernel(tile, coef, cols_t, rows_t, table, wide, mixed_rows):
    wide[...] = jnp.zeros_like(wide)
    mixed_rows[...] = jnp.zeros_like(mixed_rows)
    wide[6 : 6 + TAPS, :] = cols_t[...].astype(jnp.float32)
    for p in range(6):
        mixed_rows[24 * p : 24 * p + TAPS, :] = rows_t[...].astype(jnp.float32) * coef[p]
    every = lax.dot_general(
        mixed_rows[...],
        wide[...],
        (((1,), (1,)), ((), ())),
        preferred_element_type=jnp.float32,
        precision=lax.Precision.HIGHEST,
    )
    taps = [every[24 * p : 24 * p + TAPS] for p in range(6)]
    lane = lax.broadcasted_iota(jnp.int32, (BAND, 128), 1)
    row = lax.broadcasted_iota(jnp.int32, (BAND, 128), 0)
    for band in range(2):
        first = tile[0] * ROWS + band * BAND
        yn = (2.0 * (first + row).astype(jnp.float32) + 1.0) / CUTOUT - 1.0
        yy = yn * yn

        def turned(i):
            v = [jnp.broadcast_to(taps[p][i : i + 1, :], (BAND, 128)) for p in range(6)]
            mixed = (v[0] + yn * v[1] + yy * v[3], v[2] + yn * v[4], v[5])
            return [
                pltpu.roll(m, (i * WINDOW) % 128, 1, stride=1, stride_axis=0) for m in mixed
            ]

        held = {}
        for column in range(DEPTH // 128):
            left = (128 * column) // WINDOW
            bound = (left + 1) * WINDOW - 128 * column
            for i in (left, left + 1):
                if i < TAPS and i not in held:
                    held[i] = turned(i)
            for q in range(3):
                other = held[left + 1][q] if left + 1 < TAPS else jnp.zeros((BAND, 128), jnp.float32)
                table[band, q * BAND : (q + 1) * BAND, column * 128 : (column + 1) * 128] = jnp.where(
                    lane < bound, held[left][q], other
                ).astype(jnp.bfloat16)
            held = {i: held[i] for i in held if i > left}


def edge_kernel(
    tile,
    image,
    mask,
    row_warp,
    coef,
    cols,
    rows,
    to_next,
    to_previous,
    good,
    coef_near,
    cols_near,
    rows_near,
    level,
    held,
    own_part,
    sems,
):
    last = ROWS - EDGE
    copies = []
    parts = [(0, EDGE), (last, EDGE)] + [(EDGE + 32 * part, 32) for part in range(3)]
    for first, count in parts[:2]:
        span = pl.ds(first, count)
        copies.append(pltpu.make_async_copy(mask.at[span], held.at[span], sems.at[len(copies)]))
    copies.append(
        pltpu.make_async_copy(image.at[pl.ds(last, EDGE)], to_next.at[pl.ds(0, EDGE)], sems.at[2])
    )
    copies.append(
        pltpu.make_async_copy(image.at[pl.ds(0, EDGE)], to_previous.at[pl.ds(0, EDGE)], sems.at[3])
    )
    for first, count in parts[2:]:
        span = pl.ds(first, count)
        copies.append(pltpu.make_async_copy(mask.at[span], held.at[span], sems.at[len(copies)]))
    own_columns = pl.ds(pl.multiple_of(tile[0] * ROWS, ROWS), ROWS)
    for source, near in (
        (coef, coef_near),
        (cols, cols_near),
        (rows, rows_near),
    ):
        copies.append(pltpu.make_async_copy(source, near, sems.at[len(copies)]))
    middle = pltpu.make_async_copy(
        row_warp.at[pl.ds(ROWS // 2, EDGE), own_columns], own_part, sems.at[len(copies)]
    )
    middle.start()
    for copy in copies:
        copy.start()
    middle.wait()
    size = jnp.abs(own_part[...].astype(jnp.float32))
    level[...] = jnp.broadcast_to(jnp.max(size, axis=(0, 1), keepdims=True), level.shape)
    for (first, count), copy in zip(parts, copies[:2] + copies[4:7]):
        copy.wait()
        span = slice(first, first + count)
        flags = jnp.where(jnp.bitwise_and(held[span, :], 3) == 3, 0.0, 1.0)
        good[span, :] = flags.astype(jnp.bfloat16)
    for copy in copies[2:4] + copies[7:]:
        copy.wait()
    send_ends(level, good, to_next.at[pl.ds(EDGE, EDGE)], to_previous.at[pl.ds(EDGE, EDGE)])


def send_ends(level, plane, to_next, to_previous):
    is_level = jnp.broadcast_to(level[:1, :1] > 0.0, (EDGE, WIDTH))
    head, tail = plane[:EDGE, :].astype(jnp.float32), plane[ROWS - EDGE :, :].astype(jnp.float32)
    to_next[...] = jnp.where(is_level, tail, head).astype(jnp.bfloat16)
    to_previous[...] = jnp.where(is_level, head, tail).astype(jnp.bfloat16)


def conv_kernel(
    tile, visit_weight, level, before, image, after, table, good, flux, to_next, to_previous, stack
):
    t = tile[0]
    for group in range(10):
        if group == 0:
            strip = jnp.where(t > 0, before[:EDGE, :].astype(jnp.float32), 0.0)
        elif group == 9:
            strip = jnp.where(t < NTILE - 1, after[:EDGE, :].astype(jnp.float32), 0.0)
        else:
            strip = image[(group - 1) * 16 : group * 16, :].astype(jnp.float32)
        strip = jnp.concatenate([strip, jnp.zeros((16, 128), jnp.float32)], axis=1)
        for i in range(TAPS):
            moved = strip if i == HALF else pltpu.roll(strip, (HALF - i) % (WIDTH + 128), 1)
            moved = moved[:, :WIDTH].astype(jnp.bfloat16)
            if group < 6:
                at = i * WINDOW + group * 16
                stack[0, at : at + 16, :] = moved
            if group >= 4:
                at = i * WINDOW + group * 16 - BAND
                stack[1, at : at + 16, :] = moved
    stack[:, USED:, :] = jnp.zeros((2, DEPTH - USED, WIDTH), jnp.bfloat16)
    scale = visit_weight[0].astype(jnp.bfloat16).astype(jnp.float32)
    for band in range(2):
        rows = slice(band * BAND, (band + 1) * BAND)
        for n in range(4):
            columns = slice(n * 256, (n + 1) * 256)
            parts = jnp.dot(
                table[band], stack[band, :, columns], preferred_element_type=jnp.float32
            )
            x = lax.broadcasted_iota(jnp.int32, (BAND, 256), 1) + n * 256
            xn = (2.0 * x.astype(jnp.float32) + 1.0) / WIDTH - 1.0
            conv = parts[:BAND] + xn * (parts[BAND : 2 * BAND] + xn * parts[2 * BAND :])
            weight = scale * good[rows, columns].astype(jnp.float32)
            flux[rows, columns] = (weight * conv).astype(jnp.bfloat16)
    send_ends(level, flux, to_next, to_previous)


def near_columns(t, level, row_warp):
    def columns(block):
        return row_warp[:, pl.ds(pl.multiple_of(lax.rem(block, NTILE) * ROWS, ROWS), ROWS)]

    is_level = jnp.broadcast_to(level[:1, :1] > 0.0, (ROWS, EDGE))

    def end(block, first_if_level):
        part = columns(block).astype(jnp.float32)
        first, last = part[:, :EDGE], part[:, ROWS - EDGE :]
        chosen = (first, last) if first_if_level else (last, first)
        return jnp.where(is_level, chosen[0], chosen[1]).astype(jnp.bfloat16)

    parts = [columns(t + 2), end(t + 1, True), end(t + 3, False)]
    return columns(t), jnp.concatenate(parts, axis=1)


def gather_rest(rest, far, after, before):
    rest[:ROWS, :] = far[...]
    rest[ROWS : ROWS + EDGE, :] = after[...]
    rest[ROWS + EDGE :, :] = before[...]


def warp_columns(rowed, col_warp):
    for n in range(4):
        low, high = max(0, 256 * n - 128), min(WIDTH, 256 * n + 384)
        yield (
            n,
            jnp.dot(
                rowed[:, low:high],
                col_warp[low:high, 256 * n : 256 * n + 256],
                preferred_element_type=jnp.float32,
            ).astype(jnp.bfloat16),
        )


def warp_weight_kernel(
    tile,
    visit_weight,
    level,
    flux,
    own,
    far,
    after,
    before,
    row_warp,
    col_warp,
    warped,
    share,
    turn,
    rest,
    rowed,
):
    near, turned = near_columns(tile[0], level, row_warp)
    share[...] = jnp.dot(near, flux[...], preferred_element_type=jnp.float32)
    turn[...] = turned
    gather_rest(rest, far, after.at[pl.ds(EDGE, EDGE)], before.at[pl.ds(EDGE, EDGE)])
    both = jnp.dot(near, own[...], preferred_element_type=jnp.float32) + jnp.dot(
        turned, rest[...], preferred_element_type=jnp.float32
    )
    scale = visit_weight[0].astype(jnp.bfloat16).astype(jnp.float32)
    rowed[...] = (scale * both).astype(jnp.bfloat16)
    for n, part in warp_columns(rowed, col_warp):
        warped[:, 256 * n : 256 * n + 256] = part


def warp_flux_kernel(
    dest_slot_in,
    share,
    turn,
    far,
    after,
    before,
    col_warp,
    warped_weight,
    notes,
    outgoing,
    rest,
    rowed,
    dest_slot,
    sem,
):
    copy = pltpu.make_async_copy(dest_slot_in, dest_slot, sem)
    copy.start()
    gather_rest(rest, far, after, before)
    rowed[...] = (
        share[...] + jnp.dot(turn[...], rest[...], preferred_element_type=jnp.float32)
    ).astype(jnp.bfloat16)
    outgoing[:, 64:, :] = notes[...]
    copy.wait()
    for n, part in warp_columns(rowed, col_warp):
        for down in range(8):
            for c in range(2):
                column = 2 * n + c
                slot = dest_slot[down * 8 + column]
                owner, at = slot // 2, pl.multiple_of(lax.rem(slot, 2) * 32, 32)
                rows = slice(down * 16, down * 16 + 16)
                outgoing[owner, pl.ds(at, 16), :] = part[rows, c * 128 : c * 128 + 128]
                outgoing[owner, pl.ds(at + 16, 16), :] = warped_weight[
                    rows, column * 128 : column * 128 + 128
                ]


def patch_kernel(arriving, values, reply, sums, more, served, note, table, sem):
    notes = arriving[0, 64:, :].astype(jnp.float32)
    for sender in range(1, 64):
        notes = notes + arriving[sender, 64:, :].astype(jnp.float32)
    note[...] = notes.astype(jnp.int32)
    copy = pltpu.make_async_copy(note, table, sem)
    copy.start()
    sums[...] = jnp.zeros_like(sums)
    more[...] = jnp.zeros_like(more)
    copy.wait()

    def add(sender, _):
        for rank in range(2):
            at = table[0, 2 * sender + rank]
            total = (sums, more)[rank]
            total[at] = total[at] + arriving[sender, rank * 32 : rank * 32 + 32, :].astype(jnp.float32)
        return 0

    lax.fori_loop(0, 64, add, 0, unroll=4)
    for block in range(NBLK):
        down, c = block // 8, block % 8
        total = sums[block] + more[block]
        value = total[:16, :] / jnp.maximum(total[16:, :], FLOOR)
        values[down * 16 : down * 16 + 16, c * 128 : c * 128 + 128] = value
        served[block] = value.astype(jnp.bfloat16)

    def serve(group, _):
        asked = [served[table[1, 8 * group + i]] for i in range(8)]
        for i in range(8):
            reply[8 * group + i] = asked[i]
        return 0

    lax.fori_loop(0, 16, serve, 0)


def difference_kernel(tmpl_slot, returned, new_science, values, coadd, difference, held, sems):
    copies = [pltpu.make_async_copy(values, coadd, sems.at[4])]
    copies[0].start()
    for down in range(8):
        rows = slice(down * 16, down * 16 + 16)
        for c in range(8):
            columns = slice(c * 128, c * 128 + 128)
            template = returned[tmpl_slot[down * 8 + c]].astype(jnp.float32)
            held[rows, columns] = new_science[rows, columns] - template
        if down % 2 == 1:
            part = pl.ds(down * 16 - 16, 32)
            copies.append(
                pltpu.make_async_copy(held.at[part], difference.at[part], sems.at[down // 2])
            )
            copies[-1].start()
    for copy in copies:
        copy.wait()


def per_device(
    visit_image,
    mask_bits,
    visit_weight,
    basis_cols,
    basis_rows,
    kernel_coef,
    row_warp,
    col_warp,
    dest_owner,
    dest_block,
    new_science,
    tmpl_owner,
    tmpl_block,
):
    f32, bf16, i32 = jnp.float32, jnp.bfloat16, jnp.int32
    struct = jax.ShapeDtypeStruct
    tile = lax.axis_index("tile").astype(i32).reshape(1)
    home = lax.axis_index("ccd").astype(i32).reshape(1)
    up = [(i, (i + 1) % NTILE) for i in range(NTILE)]
    down = [(i, (i + 3) % NTILE) for i in range(NTILE)]
    across = [(i, (i + 2) % NTILE) for i in range(NTILE)]

    to_next, to_previous, good, coef, cols_t, rows_t, level = call(
        edge_kernel,
        (
            struct((2 * EDGE, WIDTH), bf16),
            struct((2 * EDGE, WIDTH), bf16),
            struct((ROWS, WIDTH), bf16),
            struct((6, 1, NB), f32),
            struct((TAPS, NB), bf16),
            struct((TAPS, NB), bf16),
            struct((8, 128), f32),
        ),
        [SMEM] + [HBM] * 6,
        (VMEM,) * 7,
        [
            pltpu.VMEM((ROWS, WIDTH), i32),
            pltpu.VMEM((EDGE, ROWS), bf16),
            pltpu.SemaphoreType.DMA((11,)),
        ],
        "edges",
        400_000,
        1_000_000,
    )(
        tile,
        in_hbm(visit_image),
        in_hbm(mask_bits),
        in_hbm(row_warp),
        in_hbm(kernel_coef.transpose(2, 0, 1)),
        in_hbm(basis_cols.T),
        in_hbm(basis_rows.T),
    )
    before = lax.ppermute(to_next, "tile", up)
    after = lax.ppermute(to_previous, "tile", down)

    dest_slot, tmpl_slot, notes = call(
        index_kernel,
        (struct((64,), i32), struct((64,), i32), struct((64, NOTE, 128), bf16)),
        [SMEM] * 5,
        (SMEM, SMEM, VMEM),
        [pltpu.SMEM((128,), i32), pltpu.SMEM((256,), i32)],
        "slots",
        2_000_000,
        1_000_000,
    )(home, dest_owner[:, 0], dest_block, tmpl_owner[:, 0], tmpl_block)

    taps = call(
        table_kernel,
        struct((2, 3 * BAND, DEPTH), bf16),
        [SMEM, VMEM, VMEM, VMEM],
        VMEM,
        [pltpu.VMEM((128, NB), f32), pltpu.VMEM((144, NB), f32)],
        "taps",
        10_000_000,
        2_000_000,
    )(tile, coef, cols_t, rows_t)
    later_good, taps = lax.optimization_barrier((good, taps))
    far_good = lax.ppermute(later_good, "tile", across)
    flux, flux_to_next, flux_to_previous = call(
        conv_kernel,
        (struct((ROWS, WIDTH), bf16),) + (struct((EDGE, WIDTH), bf16),) * 2,
        [SMEM] * 2 + [VMEM] * 6,
        (VMEM,) * 3,
        [pltpu.VMEM((2, DEPTH, WIDTH), bf16)],
        "matching",
        2 * 2 * 192 * DEPTH * WIDTH,
        3_000_000,
    )(tile, visit_weight, level, before, visit_image, after, taps, good)
    far_flux = lax.ppermute(flux, "tile", across)
    after_flux = lax.ppermute(flux_to_previous, "tile", down)
    before_flux = lax.ppermute(flux_to_next, "tile", up)
    reach = ROWS + 2 * EDGE
    scratch = [pltpu.VMEM((reach, WIDTH), bf16), pltpu.VMEM((ROWS, WIDTH), bf16)]
    warped_weight, share, turn = call(
        warp_weight_kernel,
        (struct((ROWS, WIDTH), bf16), struct((ROWS, WIDTH), f32), struct((ROWS, reach), bf16)),
        [SMEM] * 2 + [VMEM] * 8,
        (VMEM,) * 3,
        scratch,
        "warp_weight",
        2 * 128 * WIDTH * WIDTH,
        4_000_000,
    )(tile, visit_weight, level, flux, good, far_good, after, before, row_warp, col_warp[0])
    outgoing = call(
        warp_flux_kernel,
        struct((64, MESSAGE, 128), bf16),
        [VMEM] * 9,
        VMEM,
        scratch + [pltpu.SMEM((64,), i32), pltpu.SemaphoreType.DMA],
        "warp_flux",
        2 * 128 * WIDTH * WIDTH,
        5_000_000,
    )(
        dest_slot,
        share,
        turn,
        far_flux,
        after_flux,
        before_flux,
        col_warp[0],
        warped_weight,
        notes,
    )
    arriving = lax.all_to_all(outgoing, "ccd", split_axis=0, concat_axis=0, tiled=True)
    values, reply = call(
        patch_kernel,
        (struct((ROWS, WIDTH), f32), struct((SLOTS, 16, 128), bf16)),
        [VMEM],
        (VMEM, VMEM),
        [
            pltpu.VMEM((NBLK + 8, 32, 128), f32),
            pltpu.VMEM((NBLK + 8, 32, 128), f32),
            pltpu.VMEM((NBLK, 16, 128), bf16),
            pltpu.VMEM((NOTE, 128), i32),
            pltpu.SMEM((NOTE, 128), i32),
            pltpu.SemaphoreType.DMA,
        ],
        "patch",
        1_000_000,
        2_000_000,
    )(arriving)
    returned = lax.all_to_all(reply, "ccd", split_axis=0, concat_axis=0, tiled=True)
    return call(
        difference_kernel,
        (struct((ROWS, WIDTH), f32),) * 2,
        [SMEM, VMEM, VMEM, VMEM],
        (HBM, HBM),
        [pltpu.VMEM((ROWS, WIDTH), f32), pltpu.SemaphoreType.DMA((5,))],
        "difference",
        1_000_000,
        3_000_000,
    )(tmpl_slot, returned, new_science, values)


def solution(mesh):
    both = P(("ccd", "tile"), None)
    return jax.shard_map(
        per_device,
        mesh=mesh,
        in_specs=(
            both,
            both,
            P("ccd"),
            P(),
            P(),
            P("ccd", None, None),
            both,
            P("ccd", None, None),
            both,
            P(("ccd", "tile")),
            both,
            both,
            P(("ccd", "tile")),
        ),
        out_specs=(both, both),
        check_vma=False,
    )
```

```python
import functools

import jax
import jax.numpy as jnp
from jax import lax
from jax.experimental import pallas as pl
from jax.experimental.pallas import tpu as pltpu
from jax.sharding import PartitionSpec as P

BLOCK_ROWS = 16
BLOCK_COLUMNS = 128
FLOOR = 1.0

ROWS = 128
WIDTH = 1024
CUTOUT = 512
NTILE = 4
NB = 31
TAPS = 21
HALF = 10
EDGE = 16
BAND = 64
WINDOW = 96
DEPTH = 2048
USED = TAPS * WINDOW
NBLK = 64
SLOTS = 128
NOTE = 8
MESSAGE = 64 + NOTE

VMEM = pl.BlockSpec(memory_space=pltpu.VMEM)
HBM = pl.BlockSpec(memory_space=pltpu.HBM)
SMEM = pl.BlockSpec(memory_space=pltpu.SMEM)


def in_hbm(array):
    return pltpu.with_memory_space_constraint(array, pltpu.HBM)


def call(body, out_shape, in_specs, out_specs, scratch, name, flops, nbytes, aliases={}):
    return pl.pallas_call(
        body,
        out_shape=out_shape,
        in_specs=in_specs,
        out_specs=out_specs,
        scratch_shapes=scratch,
        name=name,
        input_output_aliases=aliases,
        compiler_params=pltpu.CompilerParams(vmem_limit_bytes=20 * 1024 * 1024),
        cost_estimate=pl.CostEstimate(flops=flops, bytes_accessed=nbytes, transcendentals=0),
    )


def index_kernel(
    home,
    dest_owner,
    dest_block,
    tmpl_owner,
    tmpl_block,
    dest_slot,
    tmpl_slot,
    notes,
    count,
    table,
):
    def clear(i, _):
        count[i] = 0
        count[64 + i] = 0
        table[4 * i] = NBLK
        table[4 * i + 1] = NBLK
        table[4 * i + 2] = 0
        table[4 * i + 3] = 0
        return 0

    lax.fori_loop(0, 64, clear, 0, unroll=8)

    def place(k, _):
        owner = dest_owner[k]
        rank = count[owner]
        count[owner] = rank + 1
        dest_slot[k] = 2 * owner + rank
        table[4 * owner + rank] = dest_block[k]
        asked = tmpl_owner[k]
        rank = count[64 + asked]
        count[64 + asked] = rank + 1
        tmpl_slot[k] = 2 * asked + rank
        table[4 * asked + 2 + rank] = tmpl_block[k]
        return 0

    lax.fori_loop(0, 64, place, 0, unroll=8)

    row = lax.broadcasted_iota(jnp.int32, (NOTE, 128), 0)
    lane = lax.broadcasted_iota(jnp.int32, (NOTE, 128), 1) - 2 * home[0]
    for patch in range(64):
        note = jnp.zeros((NOTE, 128), jnp.int32)
        for kind in range(2):
            for rank in range(2):
                here = (row == kind) & (lane == rank)
                note = jnp.where(here, table[4 * patch + 2 * kind + rank], note)
        notes[patch] = note.astype(jnp.float32).astype(jnp.bfloat16)


def table_kernel(tile, coef, cols_t, rows_t, table, wide, mixed_rows):
    wide[...] = jnp.zeros_like(wide)
    mixed_rows[...] = jnp.zeros_like(mixed_rows)
    wide[6 : 6 + TAPS, :] = cols_t[...].astype(jnp.float32)
    for p in range(6):
        mixed_rows[24 * p : 24 * p + TAPS, :] = rows_t[...].astype(jnp.float32) * coef[p]
    every = lax.dot_general(
        mixed_rows[...],
        wide[...],
        (((1,), (1,)), ((), ())),
        preferred_element_type=jnp.float32,
        precision=lax.Precision.HIGHEST,
    )
    taps = [every[24 * p : 24 * p + TAPS] for p in range(6)]
    lane = lax.broadcasted_iota(jnp.int32, (BAND, 128), 1)
    row = lax.broadcasted_iota(jnp.int32, (BAND, 128), 0)
    for band in range(2):
        first = tile[0] * ROWS + band * BAND
        yn = (2.0 * (first + row).astype(jnp.float32) + 1.0) / CUTOUT - 1.0
        yy = yn * yn

        def turned(i):
            v = [jnp.broadcast_to(taps[p][i : i + 1, :], (BAND, 128)) for p in range(6)]
            mixed = (v[0] + yn * v[1] + yy * v[3], v[2] + yn * v[4], v[5])
            return [
                pltpu.roll(m, (i * WINDOW) % 128, 1, stride=1, stride_axis=0) for m in mixed
            ]

        held = {}
        for column in range(DEPTH // 128):
            left = (128 * column) // WINDOW
            bound = (left + 1) * WINDOW - 128 * column
            for i in (left, left + 1):
                if i < TAPS and i not in held:
                    held[i] = turned(i)
            for q in range(3):
                other = held[left + 1][q] if left + 1 < TAPS else jnp.zeros((BAND, 128), jnp.float32)
                table[band, q * BAND : (q + 1) * BAND, column * 128 : (column + 1) * 128] = jnp.where(
                    lane < bound, held[left][q], other
                ).astype(jnp.bfloat16)
            held = {i: held[i] for i in held if i > left}


def edge_kernel(
    tile,
    image,
    mask,
    row_warp,
    coef,
    cols,
    rows,
    to_next,
    to_previous,
    good,
    coef_near,
    cols_near,
    rows_near,
    level,
    held,
    own_part,
    sems,
):
    last = ROWS - EDGE
    copies = []
    parts = [(0, EDGE), (last, EDGE)] + [(EDGE + 32 * part, 32) for part in range(3)]
    for first, count in parts[:2]:
        span = pl.ds(first, count)
        copies.append(pltpu.make_async_copy(mask.at[span], held.at[span], sems.at[len(copies)]))
    copies.append(
        pltpu.make_async_copy(image.at[pl.ds(last, EDGE)], to_next.at[pl.ds(0, EDGE)], sems.at[2])
    )
    copies.append(
        pltpu.make_async_copy(image.at[pl.ds(0, EDGE)], to_previous.at[pl.ds(0, EDGE)], sems.at[3])
    )
    for first, count in parts[2:]:
        span = pl.ds(first, count)
        copies.append(pltpu.make_async_copy(mask.at[span], held.at[span], sems.at[len(copies)]))
    own_columns = pl.ds(pl.multiple_of(tile[0] * ROWS, ROWS), ROWS)
    for source, near in (
        (coef, coef_near),
        (cols, cols_near),
        (rows, rows_near),
    ):
        copies.append(pltpu.make_async_copy(source, near, sems.at[len(copies)]))
    middle = pltpu.make_async_copy(
        row_warp.at[pl.ds(ROWS // 2, EDGE), own_columns], own_part, sems.at[len(copies)]
    )
    middle.start()
    for copy in copies:
        copy.start()
    middle.wait()
    size = jnp.abs(own_part[...].astype(jnp.float32))
    level[...] = jnp.broadcast_to(jnp.max(size, axis=(0, 1), keepdims=True), level.shape)
    for (first, count), copy in zip(parts, copies[:2] + copies[4:7]):
        copy.wait()
        span = slice(first, first + count)
        flags = jnp.where(jnp.bitwise_and(held[span, :], 3) == 3, 0.0, 1.0)
        good[span, :] = flags.astype(jnp.bfloat16)
    for copy in copies[2:4] + copies[7:]:
        copy.wait()
    send_ends(level, good, to_next.at[pl.ds(EDGE, EDGE)], to_previous.at[pl.ds(EDGE, EDGE)])


def send_ends(level, plane, to_next, to_previous):
    is_level = jnp.broadcast_to(level[:1, :1] > 0.0, (EDGE, WIDTH))
    head, tail = plane[:EDGE, :].astype(jnp.float32), plane[ROWS - EDGE :, :].astype(jnp.float32)
    to_next[...] = jnp.where(is_level, tail, head).astype(jnp.bfloat16)
    to_previous[...] = jnp.where(is_level, head, tail).astype(jnp.bfloat16)


def conv_kernel(
    tile, visit_weight, level, before, image, after, table, good, flux, to_next, to_previous, stack
):
    t = tile[0]
    for group in range(10):
        if group == 0:
            strip = jnp.where(t > 0, before[:EDGE, :].astype(jnp.float32), 0.0)
        elif group == 9:
            strip = jnp.where(t < NTILE - 1, after[:EDGE, :].astype(jnp.float32), 0.0)
        else:
            strip = image[(group - 1) * 16 : group * 16, :].astype(jnp.float32)
        strip = jnp.concatenate([strip, jnp.zeros((16, 128), jnp.float32)], axis=1)
        for i in range(TAPS):
            moved = strip if i == HALF else pltpu.roll(strip, (HALF - i) % (WIDTH + 128), 1)
            moved = moved[:, :WIDTH].astype(jnp.bfloat16)
            if group < 6:
                at = i * WINDOW + group * 16
                stack[0, at : at + 16, :] = moved
            if group >= 4:
                at = i * WINDOW + group * 16 - BAND
                stack[1, at : at + 16, :] = moved
    stack[:, USED:, :] = jnp.zeros((2, DEPTH - USED, WIDTH), jnp.bfloat16)
    scale = visit_weight[0].astype(jnp.bfloat16).astype(jnp.float32)
    for band in range(2):
        rows = slice(band * BAND, (band + 1) * BAND)
        for n in range(4):
            columns = slice(n * 256, (n + 1) * 256)
            parts = jnp.dot(
                table[band], stack[band, :, columns], preferred_element_type=jnp.float32
            )
            x = lax.broadcasted_iota(jnp.int32, (BAND, 256), 1) + n * 256
            xn = (2.0 * x.astype(jnp.float32) + 1.0) / WIDTH - 1.0
            conv = parts[:BAND] + xn * (parts[BAND : 2 * BAND] + xn * parts[2 * BAND :])
            weight = scale * good[rows, columns].astype(jnp.float32)
            flux[rows, columns] = (weight * conv).astype(jnp.bfloat16)
    send_ends(level, flux, to_next, to_previous)


def near_columns(t, level, row_warp):
    def columns(block):
        return row_warp[:, pl.ds(pl.multiple_of(lax.rem(block, NTILE) * ROWS, ROWS), ROWS)]

    is_level = jnp.broadcast_to(level[:1, :1] > 0.0, (ROWS, EDGE))

    def end(block, first_if_level):
        part = columns(block).astype(jnp.float32)
        first, last = part[:, :EDGE], part[:, ROWS - EDGE :]
        chosen = (first, last) if first_if_level else (last, first)
        return jnp.where(is_level, chosen[0], chosen[1]).astype(jnp.bfloat16)

    parts = [columns(t + 2), end(t + 1, True), end(t + 3, False)]
    return columns(t), jnp.concatenate(parts, axis=1)


def gather_rest(rest, far, after, before):
    rest[:ROWS, :] = far[...]
    rest[ROWS : ROWS + EDGE, :] = after[...]
    rest[ROWS + EDGE :, :] = before[...]


def warp_columns(rowed, col_warp):
    for n in range(4):
        low, high = max(0, 256 * n - 128), min(WIDTH, 256 * n + 384)
        yield (
            n,
            jnp.dot(
                rowed[:, low:high],
                col_warp[low:high, 256 * n : 256 * n + 256],
                preferred_element_type=jnp.float32,
            ).astype(jnp.bfloat16),
        )


def place_blocks(n, part, dest_slot, plane, outgoing):
    for down in range(8):
        for c in range(2):
            slot = dest_slot[down * 8 + 2 * n + c]
            owner, at = slot // 2, pl.multiple_of(lax.rem(slot, 2) * 32 + plane * 16, 16)
            block = part[down * 16 : down * 16 + 16, c * 128 : c * 128 + 128]
            outgoing[owner, pl.ds(at, 16), :] = block


def warp_weight_kernel(
    tile,
    visit_weight,
    dest_slot,
    level,
    flux,
    own,
    far,
    after,
    before,
    row_warp,
    col_warp,
    notes,
    outgoing,
    share,
    turn,
    rest,
    rowed,
):
    near, turned = near_columns(tile[0], level, row_warp)
    share[...] = jnp.dot(near, flux[...], preferred_element_type=jnp.float32)
    turn[...] = turned
    gather_rest(rest, far, after.at[pl.ds(EDGE, EDGE)], before.at[pl.ds(EDGE, EDGE)])
    both = jnp.dot(near, own[...], preferred_element_type=jnp.float32) + jnp.dot(
        turned, rest[...], preferred_element_type=jnp.float32
    )
    scale = visit_weight[0].astype(jnp.bfloat16).astype(jnp.float32)
    rowed[...] = (scale * both).astype(jnp.bfloat16)
    for n, part in warp_columns(rowed, col_warp):
        place_blocks(n, part, dest_slot, 1, outgoing)
    outgoing[:, 64:, :] = notes[...]


def warp_flux_kernel(
    dest_slot_in,
    share,
    turn,
    far,
    after,
    before,
    col_warp,
    begun,
    outgoing,
    rest,
    rowed,
    dest_slot,
    sem,
):
    copy = pltpu.make_async_copy(dest_slot_in, dest_slot, sem)
    copy.start()
    gather_rest(rest, far, after, before)
    rowed[...] = (
        share[...] + jnp.dot(turn[...], rest[...], preferred_element_type=jnp.float32)
    ).astype(jnp.bfloat16)
    copy.wait()
    for n, part in warp_columns(rowed, col_warp):
        place_blocks(n, part, dest_slot, 0, outgoing)


def patch_kernel(arriving, values, reply, sums, more, served, note, table, sem):
    notes = arriving[0, 64:, :].astype(jnp.float32)
    for sender in range(1, 64):
        notes = notes + arriving[sender, 64:, :].astype(jnp.float32)
    note[...] = notes.astype(jnp.int32)
    copy = pltpu.make_async_copy(note, table, sem)
    copy.start()
    sums[...] = jnp.zeros_like(sums)
    more[...] = jnp.zeros_like(more)
    copy.wait()

    def add(sender, _):
        for rank in range(2):
            at = table[0, 2 * sender + rank]
            total = (sums, more)[rank]
            total[at] = total[at] + arriving[sender, rank * 32 : rank * 32 + 32, :].astype(jnp.float32)
        return 0

    lax.fori_loop(0, 64, add, 0, unroll=4)
    for block in range(NBLK):
        down, c = block // 8, block % 8
        total = sums[block] + more[block]
        value = total[:16, :] / jnp.maximum(total[16:, :], FLOOR)
        values[down * 16 : down * 16 + 16, c * 128 : c * 128 + 128] = value
        served[block] = value.astype(jnp.bfloat16)

    def serve(group, _):
        asked = [served[table[1, 8 * group + i]] for i in range(8)]
        for i in range(8):
            reply[8 * group + i] = asked[i]
        return 0

    lax.fori_loop(0, 16, serve, 0)


def difference_kernel(tmpl_slot, returned, new_science, values, coadd, difference, held, sems):
    copies = [pltpu.make_async_copy(values, coadd, sems.at[4])]
    copies[0].start()
    for down in range(8):
        rows = slice(down * 16, down * 16 + 16)
        for c in range(8):
            columns = slice(c * 128, c * 128 + 128)
            template = returned[tmpl_slot[down * 8 + c]].astype(jnp.float32)
            held[rows, columns] = new_science[rows, columns] - template
        if down % 2 == 1:
            part = pl.ds(down * 16 - 16, 32)
            copies.append(
                pltpu.make_async_copy(held.at[part], difference.at[part], sems.at[down // 2])
            )
            copies[-1].start()
    for copy in copies:
        copy.wait()


def per_device(
    visit_image,
    mask_bits,
    visit_weight,
    basis_cols,
    basis_rows,
    kernel_coef,
    row_warp,
    col_warp,
    dest_owner,
    dest_block,
    new_science,
    tmpl_owner,
    tmpl_block,
):
    f32, bf16, i32 = jnp.float32, jnp.bfloat16, jnp.int32
    struct = jax.ShapeDtypeStruct
    tile = lax.axis_index("tile").astype(i32).reshape(1)
    home = lax.axis_index("ccd").astype(i32).reshape(1)
    up = [(i, (i + 1) % NTILE) for i in range(NTILE)]
    down = [(i, (i + 3) % NTILE) for i in range(NTILE)]
    across = [(i, (i + 2) % NTILE) for i in range(NTILE)]

    to_next, to_previous, good, coef, cols_t, rows_t, level = call(
        edge_kernel,
        (
            struct((2 * EDGE, WIDTH), bf16),
            struct((2 * EDGE, WIDTH), bf16),
            struct((ROWS, WIDTH), bf16),
            struct((6, 1, NB), f32),
            struct((TAPS, NB), bf16),
            struct((TAPS, NB), bf16),
            struct((8, 128), f32),
        ),
        [SMEM] + [HBM] * 6,
        (VMEM,) * 7,
        [
            pltpu.VMEM((ROWS, WIDTH), i32),
            pltpu.VMEM((EDGE, ROWS), bf16),
            pltpu.SemaphoreType.DMA((11,)),
        ],
        "edges",
        400_000,
        1_000_000,
    )(
        tile,
        in_hbm(visit_image),
        in_hbm(mask_bits),
        in_hbm(row_warp),
        in_hbm(kernel_coef.transpose(2, 0, 1)),
        in_hbm(basis_cols.T),
        in_hbm(basis_rows.T),
    )
    before = lax.ppermute(to_next, "tile", up)
    after = lax.ppermute(to_previous, "tile", down)

    dest_slot, tmpl_slot, notes = call(
        index_kernel,
        (struct((64,), i32), struct((64,), i32), struct((64, NOTE, 128), bf16)),
        [SMEM] * 5,
        (SMEM, SMEM, VMEM),
        [pltpu.SMEM((128,), i32), pltpu.SMEM((256,), i32)],
        "slots",
        2_000_000,
        1_000_000,
    )(home, dest_owner[:, 0], dest_block, tmpl_owner[:, 0], tmpl_block)

    taps = call(
        table_kernel,
        struct((2, 3 * BAND, DEPTH), bf16),
        [SMEM, VMEM, VMEM, VMEM],
        VMEM,
        [pltpu.VMEM((128, NB), f32), pltpu.VMEM((144, NB), f32)],
        "taps",
        10_000_000,
        2_000_000,
    )(tile, coef, cols_t, rows_t)
    later_good, taps = lax.optimization_barrier((good, taps))
    far_good = lax.ppermute(later_good, "tile", across)
    flux, flux_to_next, flux_to_previous = call(
        conv_kernel,
        (struct((ROWS, WIDTH), bf16),) + (struct((EDGE, WIDTH), bf16),) * 2,
        [SMEM] * 2 + [VMEM] * 6,
        (VMEM,) * 3,
        [pltpu.VMEM((2, DEPTH, WIDTH), bf16)],
        "matching",
        2 * 2 * 192 * DEPTH * WIDTH,
        3_000_000,
    )(tile, visit_weight, level, before, visit_image, after, taps, good)
    far_flux = lax.ppermute(flux, "tile", across)
    after_flux = lax.ppermute(flux_to_previous, "tile", down)
    before_flux = lax.ppermute(flux_to_next, "tile", up)
    reach = ROWS + 2 * EDGE
    scratch = [pltpu.VMEM((reach, WIDTH), bf16), pltpu.VMEM((ROWS, WIDTH), bf16)]
    begun, share, turn = call(
        warp_weight_kernel,
        (struct((64, MESSAGE, 128), bf16), struct((ROWS, WIDTH), f32), struct((ROWS, reach), bf16)),
        [SMEM] * 3 + [VMEM] * 9,
        (VMEM,) * 3,
        scratch,
        "warp_weight",
        2 * 128 * WIDTH * WIDTH,
        4_000_000,
    )(
        tile,
        visit_weight,
        dest_slot,
        level,
        flux,
        good,
        far_good,
        after,
        before,
        row_warp,
        col_warp[0],
        notes,
    )
    outgoing = call(
        warp_flux_kernel,
        struct((64, MESSAGE, 128), bf16),
        [VMEM] * 8,
        VMEM,
        scratch + [pltpu.SMEM((64,), i32), pltpu.SemaphoreType.DMA],
        "warp_flux",
        2 * 128 * WIDTH * WIDTH,
        5_000_000,
        {7: 0},
    )(
        dest_slot,
        share,
        turn,
        far_flux,
        after_flux,
        before_flux,
        col_warp[0],
        begun,
    )
    arriving = lax.all_to_all(outgoing, "ccd", split_axis=0, concat_axis=0, tiled=True)
    values, reply = call(
        patch_kernel,
        (struct((ROWS, WIDTH), f32), struct((SLOTS, 16, 128), bf16)),
        [VMEM],
        (VMEM, VMEM),
        [
            pltpu.VMEM((NBLK + 8, 32, 128), f32),
            pltpu.VMEM((NBLK + 8, 32, 128), f32),
            pltpu.VMEM((NBLK, 16, 128), bf16),
            pltpu.VMEM((NOTE, 128), i32),
            pltpu.SMEM((NOTE, 128), i32),
            pltpu.SemaphoreType.DMA,
        ],
        "patch",
        1_000_000,
        2_000_000,
    )(arriving)
    returned = lax.all_to_all(reply, "ccd", split_axis=0, concat_axis=0, tiled=True)
    return call(
        difference_kernel,
        (struct((ROWS, WIDTH), f32),) * 2,
        [SMEM, VMEM, VMEM, VMEM],
        (HBM, HBM),
        [pltpu.VMEM((ROWS, WIDTH), f32), pltpu.SemaphoreType.DMA((5,))],
        "difference",
        1_000_000,
        3_000_000,
    )(tmpl_slot, returned, new_science, values)


def solution(mesh):
    both = P(("ccd", "tile"), None)
    return jax.shard_map(
        per_device,
        mesh=mesh,
        in_specs=(
            both,
            both,
            P("ccd"),
            P(),
            P(),
            P("ccd", None, None),
            both,
            P("ccd", None, None),
            both,
            P(("ccd", "tile")),
            both,
            both,
            P(("ccd", "tile")),
        ),
        out_specs=(both, both),
        check_vma=False,
    )
```
